256 devices in a mesh: dp: 8 (over z), ctx: 32 (over y, x, core).
Axes of the slice: x: 4, y: 4, z: 8, core: 2. Of those that a mesh axis runs over, the one named last changes fastest.
Arguments:
- queries: bfloat16 [8, 4096, 16, 128], P('dp', 'ctx'), may hold values from -6 to 6
- key_rows: bfloat16 [8, 4096, 16, 128], P('dp', 'ctx'), may hold values from -6 to 6
- value_rows: bfloat16 [8, 4096, 16, 128], P('dp', 'ctx'), may hold values from -6 to 6
- attn_out: bfloat16 [8, 4096, 16, 128], P('dp', 'ctx'), may hold values from -6 to 6
- out_grad: bfloat16 [8, 4096, 16, 128], P('dp', 'ctx'), may hold values from -6 to 6
- log_sums: float32 [8, 16, 4096], P('dp', None, 'ctx'), may hold values from 5 to 7
- chosen: int32 [8, 32, 16, 3], P('dp', 'ctx'), may hold values from 0 to 31, as said below
- inputs: bfloat16 [8, 4096, 2048], P('dp', 'ctx'), may hold values from -6 to 6
Outputs:
- query_grad: bfloat16 [8, 4096, 16, 128], P('dp', 'ctx')
- key_grad: bfloat16 [8, 4096, 16, 128], P('dp', 'ctx')
- value_grad: bfloat16 [8, 4096, 16, 128], P('dp', 'ctx')
- weight_grad: float32 [2048, 2048], P(('dp', 'ctx'))
The draws below stay inside these ranges and needn't reach their ends.
Inputs may be any that keep to these rules, and one draw needn't show every extreme that they name: `chosen`: within one query block and head the entries name different key blocks; each entry is at most the query block's own index i, and is below i for at most min(3, i) of each head's entries. No key block is named by more than 2 heads of one query block.
All inputs are finite; a program needn't handle non-finite values.
Results may differ from the reference program's by a relative error of at most 0.006.
Values may be sent and summed in bfloat16 or wider, within the bound.
A program may use at most 128 MiB of HBM per device.

```python
import jax
import jax.numpy as jnp
from jax import lax

HEADS = 16
HD = 128
DW = 2048
TOPK = 3
CAP = 2
BLK = 128
NB = 32
SEQ = 4096
BATCH = 8


def draw_chosen(key, part):
    key = jax.random.fold_in(key, 7)

    def one_block(block_key, block_index):
        order_key, head_key = jax.random.split(block_key)
        others = jax.random.permutation(order_key, NB - 1).astype(jnp.int32) + 1
        ranked = jnp.argsort(jnp.where(others < block_index, 0, 1).astype(jnp.int32), stable=True)
        earlier = jnp.concatenate([jnp.zeros((1,), jnp.int32), others[ranked]])
        head_order = jax.random.permutation(head_key, HEADS).astype(jnp.int32)
        per_head = jnp.minimum(TOPK, block_index)
        spread = jnp.maximum(block_index, 1)
        slot_ids = jnp.arange(TOPK, dtype=jnp.int32)[None, :]
        tickets = jnp.arange(HEADS, dtype=jnp.int32)[:, None] * per_head + slot_ids
        usable = (slot_ids < per_head) & (tickets < block_index * CAP)
        picked = jnp.where(usable, earlier[tickets % spread], block_index)
        return jnp.zeros((HEADS, TOPK), jnp.int32).at[head_order].set(picked)
    block_keys = jax.random.split(key, BATCH * NB)
    block_ids = jnp.tile(jnp.arange(NB, dtype=jnp.int32), BATCH)
    return jax.vmap(one_block)(block_keys, block_ids).reshape(BATCH, NB, HEADS, TOPK)


def spiked(result, stream_key, source, target, blocks, factor):
    owner, partner = [(jnp.arange(result.shape[position]) // (result.shape[position] // blocks)).reshape([-1 if axis == position else 1 for axis in range(result.ndim)]) for position in (source, target)]
    chosen = jax.random.permutation(stream_key, blocks)[partner]
    strong = (owner == chosen) | (owner == (partner + blocks // 2) % blocks)
    return jnp.where(strong, factor * result, result)


def level_of(key, extent, pieces, low, high):
    def one(dim, blocks):
        steps = jax.random.uniform(jax.random.fold_in(jax.random.fold_in(key, 6), dim), (blocks,), jnp.float32, low / len(pieces), high / len(pieces))
        return jnp.repeat(jnp.exp(steps), extent[dim] // blocks).reshape((-1,) + (1,) * (len(extent) - dim - 1))

    factor_of = one(*pieces[0])
    for cut in pieces[1:]:
        factor_of = factor_of * one(*cut)
    return factor_of


def bell_draw(stream_key, extent, scale, bound, shards=(), kind=jnp.bfloat16):
    gain = level_of(stream_key, extent, shards, -0.22, 0.18) if shards else 1.0
    entries = jax.random.normal(stream_key, extent, jnp.float32) * scale * gain
    return jnp.minimum(jnp.maximum(entries, -bound), bound).astype(kind)


def heavy_noise(stream_key, dims, width, limit, shards, heavy, kind=jnp.bfloat16):
    result = width * jax.random.normal(stream_key, dims, jnp.float32)
    if shards:
        result = result * level_of(stream_key, dims, shards, -0.22, 0.18)
    return jnp.clip(spiked(result, jax.random.fold_in(stream_key, 3), *heavy), -limit, limit).astype(kind)


def setup_inputs(seed: int = 0) -> dict:
    splits = jax.random.split(jax.random.key(seed), 9)
    queries = bell_draw(splits[0], (BATCH, SEQ, HEADS, HD), 1.0, 6.0, ((0, 8), (1, 32)))
    key_rows = bell_draw(splits[1], (BATCH, SEQ, HEADS, HD), 1.0, 6.0, ((0, 8), (1, 32)))
    value_rows = bell_draw(splits[2], (BATCH, SEQ, HEADS, HD), 1.0, 6.0, ((0, 8), (1, 32)))
    attn_out = bell_draw(splits[3], (BATCH, SEQ, HEADS, HD), 1.0, 6.0, ((0, 8), (1, 32)))
    out_grad = bell_draw(splits[4], (BATCH, SEQ, HEADS, HD), 1.0, 6.0, ((0, 8), (1, 32)))
    log_sums = jnp.clip(5.0 + 2.0 * jax.random.uniform(splits[5], (BATCH, HEADS, SEQ), jnp.float32) ** level_of(splits[5], (BATCH, HEADS, SEQ), ((0, 8), (2, 32)), -0.2, 0.2), 5.0, 7.0)
    chosen = draw_chosen(jax.random.fold_in(splits[8], 71), 0)
    inputs = heavy_noise(splits[7], (BATCH, SEQ, DW), 1.0, 6.0, ((0, 8), (1, 32)), (1, 2, 32, 2.75))
    return {"queries": queries, "key_rows": key_rows, "value_rows": value_rows, "attn_out": attn_out, "out_grad": out_grad, "log_sums": log_sums, "chosen": chosen, "inputs": inputs}


def reference(queries, key_rows, value_rows, attn_out, out_grad, log_sums, chosen, inputs):
    softmax_scale = HD ** -0.5
    positions = jnp.arange(BLK, dtype=jnp.int32)
    causal = (positions[:, None] >= positions[None, :]).astype(jnp.float32)
    window = jnp.concatenate([causal[None], jnp.ones((TOPK, BLK, BLK), jnp.float32)], 0)
    head_index = jnp.arange(HEADS, dtype=jnp.int32)[:, None]
    query_list = []
    key_list = []
    value_list = []
    weight_grad = jnp.zeros((DW, HEADS * HD), jnp.float32)
    for sequence in range(BATCH):
        def by_head(array):
            return array[sequence].reshape(NB, BLK, HEADS, HD).transpose(2, 0, 1, 3).astype(jnp.float32)

        query_heads = by_head(queries)
        key_heads = by_head(key_rows)
        value_heads = by_head(value_rows)
        grad_heads = by_head(out_grad)
        output_heads = by_head(attn_out)
        delta_all = jnp.sum(grad_heads * output_heads, -1)
        lse_heads = log_sums[sequence].reshape(HEADS, NB, BLK)

        def visit(totals, current):
            key_total, value_total = totals
            picks, block_index = current
            targets = jnp.concatenate([jnp.full((HEADS, 1), block_index, jnp.int32), picks.astype(jnp.int32)], 1)
            keep = jnp.concatenate([jnp.ones((HEADS, 1), jnp.float32), (picks < block_index).astype(jnp.float32)], 1)
            key_sel = key_heads[head_index, targets]
            value_sel = value_heads[head_index, targets]
            query_now = lax.dynamic_index_in_dim(query_heads, block_index, 1, keepdims=False)
            grad_now = lax.dynamic_index_in_dim(grad_heads, block_index, 1, keepdims=False)
            lse_now = lax.dynamic_index_in_dim(lse_heads, block_index, 1, keepdims=False)
            delta_now = lax.dynamic_index_in_dim(delta_all, block_index, 1, keepdims=False)
            scores = jnp.einsum("hqd,hjkd->hjqk", query_now, key_sel) * softmax_scale
            allowed = window[None] * keep[:, :, None, None]
            probs = jnp.where(allowed > 0, jnp.exp(scores - lse_now[:, None, :, None]), 0.0)
            probs_low = lax.optimization_barrier(probs.astype(jnp.bfloat16)).astype(jnp.float32)
            dprobs = jnp.einsum("hqd,hjkd->hjqk", grad_now, value_sel)
            dscores = probs * (dprobs - delta_now[:, None, :, None])
            dscores = lax.optimization_barrier(dscores.astype(jnp.bfloat16)).astype(jnp.float32)
            partials = softmax_scale * jnp.einsum("hjqk,hjkd->hjqd", dscores, key_sel)
            remote = lax.optimization_barrier(partials[:, 1:].astype(jnp.bfloat16)).astype(jnp.float32)
            query_now_grad = partials[:, 0] + jnp.sum(remote, 1)
            key_part = softmax_scale * jnp.einsum("hjqk,hqd->hjkd", dscores, query_now)
            value_part = jnp.einsum("hjqk,hqd->hjkd", probs_low, grad_now)
            key_total = key_total.at[head_index, targets].add(key_part)
            value_total = value_total.at[head_index, targets].add(value_part)
            return (key_total, value_total), query_now_grad

        zero_state = jnp.zeros((HEADS, NB, BLK, HD), jnp.float32)
        block_ids = jnp.arange(NB, dtype=jnp.int32)
        (key_total, value_total), query_blocks = lax.scan(visit, (zero_state, zero_state), (chosen[sequence], block_ids))
        query_done = query_blocks.transpose(0, 2, 1, 3).reshape(SEQ, HEADS, HD).astype(jnp.bfloat16)
        query_list.append(query_done)
        key_list.append(key_total.transpose(1, 2, 0, 3).reshape(SEQ, HEADS, HD).astype(jnp.bfloat16))
        value_list.append(value_total.transpose(1, 2, 0, 3).reshape(SEQ, HEADS, HD).astype(jnp.bfloat16))
        weight_grad = weight_grad + jnp.dot(inputs[sequence].T, query_done.reshape(SEQ, HEADS * HD), preferred_element_type=jnp.float32)
    return jnp.stack(query_list), jnp.stack(key_list), jnp.stack(value_list), weight_grad
```

```python
import functools

import jax
import jax.numpy as jnp
from jax import lax
from jax.experimental import pallas as pl
from jax.experimental.pallas import tpu as pltpu
from jax.sharding import PartitionSpec as P

CAP = 2
MESH = pl.DeviceIdType.MESH
DEAD = 1e30
NT = (((1,), (1,)), ((), ()))
NN = (((1,), (0,)), ((), ()))
TN = (((0,), (0,)), ((), ()))


def mm(a, b, dims):
    return lax.dot_general(a, b, dims, preferred_element_type=jnp.float32)


def pair_grads(query, grad, key, value, lse, delta, scale, keep=None):
    scores = mm(key, query, NT) * scale
    probs = jnp.exp(scores - lse)
    if keep is not None:
        probs = jnp.where(keep, probs, 0.0)
    dprobs = mm(value, grad, NT)
    dscores = (probs * (dprobs - delta)).astype(jnp.bfloat16)
    query_part = mm(dscores, key, TN) * scale
    key_part = mm(dscores, query, NN) * scale
    value_part = mm(probs.astype(jnp.bfloat16), grad, NN)
    return query_part, key_part, value_part


def kernel(
    nd,
    nc,
    q_ref,
    k_ref,
    v_ref,
    g_ref,
    x_ref,
    lse_ref,
    delta_ref,
    ids_ref,
    head_ref,
    live_ref,
    pos_ref,
    qg_ref,
    dk_ref,
    dv_ref,
    wg_ref,
    ids_in,
    ids_smem,
    last_smem,
    fwd_out,
    fwd_in,
    stat_out,
    stat_in,
    ret_out,
    ret_in,
    own_q,
    arena_k,
    arena_v,
    x_all,
    qg_all,
    w_out,
    w_in,
    w_sum,
    w_fin,
    local_sem,
    id_send,
    id_recv,
    fwd_send,
    fwd_recv,
    stat_send,
    stat_recv,
    ret_send,
    ret_recv,
    up_send,
    up_recv,
    down_send,
    down_recv,
    sib_send,
    sib_recv,
    qg_send,
    qg_recv,
    w_send,
    w_recv,
    f_send,
    f_recv,
):
    heads, rows, depth = q_ref.shape
    scale = depth ** (-0.5)
    width = x_ref.shape[1]
    span = width // nd
    me = lax.axis_index("ctx")
    zd = lax.axis_index("dp")
    core = lax.rem(me, 2)
    chip = me // 2
    chips = nc // 2
    mine = 2 * zd + core

    def peer(j):
        return {"dp": zd, "ctx": j}

    def group_peer(t):
        return {"dp": t // 2, "ctx": 2 * chip + lax.rem(t, 2)}

    barrier = pltpu.get_barrier_semaphore()

    @pl.loop(0, nc)
    def _(j):
        @pl.when(j != me)
        def _():
            pl.semaphore_signal(barrier, inc=1, device_id=peer(j), device_id_type=MESH)

    @pl.loop(0, 2 * nd)
    def _(t):
        @pl.when(t // 2 != zd)
        def _():
            pl.semaphore_signal(barrier, inc=1, device_id=group_peer(t), device_id_type=MESH)

    def x_rows(shard, which):
        return pl.ds(pl.multiple_of((2 * shard + which) * rows, rows), rows)

    seat = pltpu.make_async_copy(x_ref, x_all.at[x_rows(zd, core)], local_sem)
    seat.start()

    @pl.loop(0, me)
    def _(j):
        for s in range(CAP):
            h = head_ref[j, s]
            fwd_out[j, s, 0] = q_ref[h]
            fwd_out[j, s, 1] = g_ref[h]
            alive = live_ref[j, s] > 0
            stat_out[j, pl.ds(s, 1), :] = jnp.where(alive, lse_ref[pl.ds(h, 1), :], DEAD)
            stat_out[j, pl.ds(CAP + s, 1), :] = delta_ref[pl.ds(h, 1), :]

    seat.wait()
    pl.semaphore_wait(barrier, (nc - 1) + 2 * (nd - 1))

    def id_copy(src, j, dst):
        return pltpu.make_async_remote_copy(
            src_ref=ids_ref,
            dst_ref=ids_in.at[src],
            send_sem=id_send.at[j],
            recv_sem=id_recv.at[src],
            device_id=peer(dst),
            device_id_type=MESH,
        )

    def fwd_copy(src, j, dst):
        return pltpu.make_async_remote_copy(
            src_ref=fwd_out.at[j],
            dst_ref=fwd_in.at[src],
            send_sem=fwd_send.at[j],
            recv_sem=fwd_recv.at[src],
            device_id=peer(dst),
            device_id_type=MESH,
        )

    def stat_copy(src, j, dst):
        return pltpu.make_async_remote_copy(
            src_ref=stat_out.at[j],
            dst_ref=stat_in.at[src],
            send_sem=stat_send.at[j],
            recv_sem=stat_recv.at[src],
            device_id=peer(dst),
            device_id_type=MESH,
        )

    def ret_copy(src, j, dst):
        return pltpu.make_async_remote_copy(
            src_ref=ret_out.at[j],
            dst_ref=ret_in.at[pl.ds(CAP * src, CAP)],
            send_sem=ret_send.at[j],
            recv_sem=ret_recv.at[src],
            device_id=peer(dst),
            device_id_type=MESH,
        )

    ups = nd // 2
    downs = nd - 1 - ups

    def up_copy(shard, s):
        return pltpu.make_async_remote_copy(
            src_ref=x_all.at[x_rows(shard, core)],
            dst_ref=x_all.at[x_rows(shard, core)],
            send_sem=up_send.at[s],
            recv_sem=up_recv.at[s],
            device_id={"dp": lax.rem(zd + 1, nd), "ctx": me},
            device_id_type=MESH,
        )

    def down_copy(shard, s):
        return pltpu.make_async_remote_copy(
            src_ref=x_all.at[x_rows(shard, core)],
            dst_ref=x_all.at[x_rows(shard, core)],
            send_sem=down_send.at[s],
            recv_sem=down_recv.at[s],
            device_id={"dp": lax.rem(zd + nd - 1, nd), "ctx": me},
            device_id_type=MESH,
        )

    def sib_copy(shard, which, n):
        return pltpu.make_async_remote_copy(
            src_ref=x_all.at[x_rows(shard, which)],
            dst_ref=x_all.at[x_rows(shard, which)],
            send_sem=sib_send.at[n],
            recv_sem=sib_recv.at[n],
            device_id=peer(2 * chip + 1 - core),
            device_id_type=MESH,
        )

    def below(s):
        return lax.rem(zd + nd - s, nd)

    def above(s):
        return lax.rem(zd + s, nd)

    def relay(k):
        if k == 0:
            up_copy(zd, 0).start()
            if downs:
                down_copy(zd, 0).start()
            sib_copy(zd, core, 0).start()
            return
        up_copy(below(k), k - 1).wait_recv()
        if k < ups:
            up_copy(below(k), k).start()
        sib_copy(below(k), core, k).start()
        if k <= downs:
            down_copy(above(k), k - 1).wait_recv()
            if k < downs:
                down_copy(above(k), k).start()
            sib_copy(above(k), core, ups + k).start()

    @pl.loop(0, me)
    def _(n):
        j = me - 1 - n
        id_copy(me, j, j).start()

    @pl.loop(0, me)
    def _(n):
        j = me - 1 - n
        stat_copy(me, j, j).start()
        fwd_copy(me, j, j).start()

    relay(0)

    key_pos = lax.broadcasted_iota(jnp.int32, (rows, rows), 0)
    query_pos = lax.broadcasted_iota(jnp.int32, (rows, rows), 1)
    causal = key_pos <= query_pos

    @pl.loop(0, heads // 2)
    def _(n):
        for s in range(2):
            h = 2 * n + s
            query_part, key_part, value_part = pair_grads(
                q_ref[h],
                g_ref[h],
                k_ref[h],
                v_ref[h],
                lse_ref[pl.ds(h, 1), :],
                delta_ref[pl.ds(h, 1), :],
                scale,
                causal,
            )
            own_q[h] = query_part
            arena_k[h] = key_part
            arena_v[h] = value_part

    for h in range(heads):
        last_smem[h] = h

    @pl.loop(me + 1, nc)
    def _(i):
        id_copy(i, i, i).wait_recv()

    to_smem = pltpu.make_async_copy(ids_in, ids_smem, local_sem)
    to_smem.start()
    to_smem.wait()

    @pl.loop(1, nc)
    def _(step):
        i = me + step

        @pl.when(i < nc)
        def _():
            stat_copy(i, i, i).wait_recv()
            fwd_copy(i, i, i).wait_recv()
            for s in range(CAP):
                h = ids_smem[i, 0, CAP * me + s]
                row = heads + CAP * i + s
                query_part, key_part, value_part = pair_grads(
                    fwd_in[i, s, 0],
                    fwd_in[i, s, 1],
                    k_ref[h],
                    v_ref[h],
                    stat_in[i, pl.ds(s, 1), :],
                    stat_in[i, pl.ds(CAP + s, 1), :],
                    scale,
                )
                ret_out[i, s] = query_part.astype(jnp.bfloat16)
                before = last_smem[h]
                arena_k[row] = arena_k[before] + key_part
                arena_v[row] = arena_v[before] + value_part
                for t in range(heads):
                    last_smem[t] = jnp.where(h == t, row, last_smem[t])
            ret_copy(me, i, i).start()

        for k in range(1, ups + 1):

            @pl.when(step == max(1, k * nc // (2 * ups)))
            def _():
                relay(k)

    @pl.loop(0, heads)
    def _(h):
        at = last_smem[h]
        dk_ref[h] = arena_k[at].astype(jnp.bfloat16)
        dv_ref[h] = arena_v[at].astype(jnp.bfloat16)

    ret_in[CAP * nc] = jnp.zeros((rows, depth), jnp.bfloat16)

    @pl.loop(0, me)
    def _(j):
        ret_copy(j, j, j).wait_recv()

    topk = pos_ref.shape[1]

    @pl.loop(0, heads)
    def _(h):
        total = own_q[h]
        for e in range(topk):
            total = total + ret_in[pos_ref[h, e]].astype(jnp.float32)
        qg_ref[h] = total.astype(jnp.bfloat16)

    def qg_copy(src, t, dst):
        return pltpu.make_async_remote_copy(
            src_ref=qg_ref.at[t],
            dst_ref=qg_all.at[pl.ds(pl.multiple_of(src * rows, rows), rows)],
            send_sem=qg_send.at[t],
            recv_sem=qg_recv.at[src],
            device_id=group_peer(dst),
            device_id_type=MESH,
        )

    @pl.loop(0, 2 * nd)
    def _(t):
        @pl.when(t != mine)
        def _():
            qg_copy(mine, t, t).start()

    qg_all[pl.ds(pl.multiple_of(mine * rows, rows), rows), :] = qg_ref[mine]

    for n in range(nd):
        shard = zd if n == 0 else (below(n) if n <= ups else above(n - ups))
        sib_copy(shard, 1 - core, n).wait_recv()

    @pl.loop(0, 2 * nd)
    def _(t):
        @pl.when(t != mine)
        def _():
            qg_copy(t, t, t).wait_recv()

    flipped = qg_all[...].T

    @pl.loop(0, nd)
    def _(r):
        part = mm(flipped, x_all[:, pl.ds(pl.multiple_of(r * span, span), span)], NN)
        w_out[:, r] = part.T.astype(jnp.bfloat16).reshape(chips, span // chips, depth)

    def w_copy(src, t, dst):
        return pltpu.make_async_remote_copy(
            src_ref=w_out.at[t],
            dst_ref=w_in.at[src],
            send_sem=w_send.at[t],
            recv_sem=w_recv.at[src],
            device_id=peer(2 * dst + core),
            device_id_type=MESH,
        )

    @pl.loop(1, chips)
    def _(n):
        t = lax.rem(chip + n, chips)
        w_copy(chip, t, t).start()

    w_in[chip] = w_out[chip]

    @pl.loop(1, chips)
    def _(n):
        t = lax.rem(chip + n, chips)
        w_copy(t, t, t).wait_recv()

    w_sum[...] = jnp.sum(w_in[...].astype(jnp.float32), 0)

    def f_copy(src, t, dst):
        return pltpu.make_async_remote_copy(
            src_ref=w_sum.at[t // 2, pl.ds(pl.multiple_of(8 * lax.rem(t, 2), 8), 8)],
            dst_ref=w_fin.at[src],
            send_sem=f_send.at[t],
            recv_sem=f_recv.at[src],
            device_id=group_peer(dst),
            device_id_type=MESH,
        )

    @pl.loop(0, 2 * nd)
    def _(t):
        @pl.when(t != mine)
        def _():
            f_copy(mine, t, t).start()

    w_fin[mine] = w_sum[zd, pl.ds(pl.multiple_of(8 * core, 8), 8), :]

    @pl.loop(0, me)
    def _(j):
        id_copy(me, j, j).wait_send()
        stat_copy(me, j, j).wait_send()
        fwd_copy(me, j, j).wait_send()

    @pl.loop(me + 1, nc)
    def _(i):
        ret_copy(me, i, i).wait_send()

    for s in range(ups):
        up_copy(zd, s).wait_send()
    for s in range(downs):
        down_copy(zd, s).wait_send()
    for n in range(nd):
        sib_copy(zd, core, n).wait_send()

    @pl.loop(1, chips)
    def _(n):
        t = lax.rem(chip + n, chips)
        w_copy(chip, t, t).wait_send()

    @pl.loop(0, 2 * nd)
    def _(t):
        @pl.when(t != mine)
        def _():
            qg_copy(mine, t, t).wait_send()
            f_copy(mine, t, t).wait_send()
            f_copy(t, t, t).wait_recv()

    for t in range(2 * nd):
        wg_ref[:, t * depth : (t + 1) * depth] = w_fin[t]


def per_device(nd, nc, queries, key_rows, value_rows, attn_out, out_grad, log_sums, chosen, inputs):
    rows, heads, depth = queries.shape[1:]
    width = inputs.shape[2]
    topk = chosen.shape[3]
    me = lax.axis_index("ctx")

    def by_head(array):
        return jnp.swapaxes(array[0], 0, 1)

    delta = jnp.sum(out_grad[0].astype(jnp.float32) * attn_out[0].astype(jnp.float32), -1).T
    flat = chosen.reshape(heads * topk)
    live = flat < me
    order = jnp.arange(heads * topk, dtype=jnp.int32)
    same = (flat[:, None] == flat[None, :]) & live[None, :] & (order[None, :] < order[:, None])
    rank = jnp.sum(same.astype(jnp.int32), -1)
    spot = jnp.where(live, CAP * flat + rank, CAP * nc)
    hit = (spot[None, :] == jnp.arange(128, dtype=jnp.int32)[:, None]) & live[None, :]
    ids = jnp.sum(jnp.where(hit, order[None, :] // topk, 0), -1)
    alive = jnp.sum(hit.astype(jnp.int32), -1)
    slots = nc * CAP
    bf16, f32 = jnp.bfloat16, jnp.float32
    chips = nc // 2
    span = width // nd
    vmem = pl.BlockSpec(memory_space=pltpu.VMEM)
    smem = pl.BlockSpec(memory_space=pltpu.SMEM)
    dma = pltpu.SemaphoreType.DMA
    ups = nd // 2
    downs = nd - 1 - ups
    outs = pl.pallas_call(
        functools.partial(kernel, nd, nc),
        out_shape=(
            jax.ShapeDtypeStruct((heads, rows, depth), bf16),
            jax.ShapeDtypeStruct((heads, rows, depth), bf16),
            jax.ShapeDtypeStruct((heads, rows, depth), bf16),
            jax.ShapeDtypeStruct((8, heads * depth), f32),
        ),
        in_specs=[vmem] * 8 + [smem] * 3,
        out_specs=(vmem,) * 4,
        scratch_shapes=[
            pltpu.VMEM((nc, 1, 128), jnp.int32),
            pltpu.SMEM((nc, 1, 128), jnp.int32),
            pltpu.SMEM((heads,), jnp.int32),
            pltpu.VMEM((nc, CAP, 2, rows, depth), bf16),
            pltpu.VMEM((nc, CAP, 2, rows, depth), bf16),
            pltpu.VMEM((nc, 8, 128), f32),
            pltpu.VMEM((nc, 8, 128), f32),
            pltpu.VMEM((nc, CAP, rows, depth), bf16),
            pltpu.VMEM((slots + 1, rows, depth), bf16),
            pltpu.VMEM((heads, rows, depth), f32),
            pltpu.VMEM((heads + slots, rows, depth), f32),
            pltpu.VMEM((heads + slots, rows, depth), f32),
            pltpu.VMEM((2 * nd * rows, width), bf16),
            pltpu.VMEM((2 * nd * rows, depth), bf16),
            pltpu.VMEM((chips, nd, span // chips, depth), bf16),
            pltpu.VMEM((chips, nd, span // chips, depth), bf16),
            pltpu.VMEM((nd, span // chips, depth), f32),
            pltpu.VMEM((2 * nd, 8, depth), f32),
            dma(()),
            dma((nc,)),
            dma((nc,)),
            dma((nc,)),
            dma((nc,)),
            dma((nc,)),
            dma((nc,)),
            dma((nc,)),
            dma((nc,)),
            dma((ups,)),
            dma((ups,)),
            dma((max(downs, 1),)),
            dma((max(downs, 1),)),
            dma((nd,)),
            dma((nd,)),
            dma((2 * nd,)),
            dma((2 * nd,)),
            dma((chips,)),
            dma((chips,)),
            dma((2 * nd,)),
            dma((2 * nd,)),
        ],
        compiler_params=pltpu.CompilerParams(
            collective_id=0, has_side_effects=True, vmem_limit_bytes=58 * 1024 * 1024
        ),
    )(
        by_head(queries),
        by_head(key_rows),
        by_head(value_rows),
        by_head(out_grad),
        inputs[0],
        log_sums[0],
        delta,
        ids[None],
        ids[:slots].reshape(nc, CAP),
        alive[:slots].reshape(nc, CAP),
        spot.reshape(heads, topk),
    )
    query_grad, key_grad, value_grad, weight_grad = outs
    return (
        jnp.swapaxes(query_grad, 0, 1)[None],
        jnp.swapaxes(key_grad, 0, 1)[None],
        jnp.swapaxes(value_grad, 0, 1)[None],
        weight_grad,
    )


def solution(mesh):
    nd, nc = mesh.shape["dp"], mesh.shape["ctx"]
    four = P("dp", "ctx", None, None)
    return jax.shard_map(
        functools.partial(per_device, nd, nc),
        mesh=mesh,
        in_specs=(four, four, four, four, four, P("dp", None, "ctx"), four, P("dp", "ctx", None)),
        out_specs=(four, four, four, P(("dp", "ctx"), None)),
        check_vma=False,
    )
```

```python
import functools

import jax
import jax.numpy as jnp
from jax import lax
from jax.experimental import pallas as pl
from jax.experimental.pallas import tpu as pltpu
from jax.sharding import PartitionSpec as P

CAP = 2
MESH = pl.DeviceIdType.MESH
DEAD = 1e30
NT = (((1,), (1,)), ((), ()))
NN = (((1,), (0,)), ((), ()))
TN = (((0,), (0,)), ((), ()))


def mm(a, b, dims):
    return lax.dot_general(a, b, dims, preferred_element_type=jnp.float32)


def pair_grads(query, grad, key, value, lse, delta, scale, keep=None):
    scores = mm(key, query, NT) * scale
    probs = jnp.exp(scores - lse)
    if keep is not None:
        probs = jnp.where(keep, probs, 0.0)
    dprobs = mm(value, grad, NT)
    dscores = (probs * (dprobs - delta)).astype(jnp.bfloat16)
    query_part = mm(dscores, key, TN) * scale
    key_part = mm(dscores, query, NN) * scale
    value_part = mm(probs.astype(jnp.bfloat16), grad, NN)
    return query_part, key_part, value_part


def kernel(
    nd,
    nc,
    q_in,
    k_in,
    v_in,
    o_in,
    g_in,
    x_ref,
    lse_ref,
    pick_ref,
    qg_out,
    dk_out,
    dv_out,
    wg_ref,
    q_ref,
    k_ref,
    v_ref,
    g_ref,
    qg_ref,
    dk_ref,
    dv_ref,
    delta_ref,
    ids_ref,
    pos_row,
    head_ref,
    pos_ref,
    ids_in,
    ids_smem,
    last_smem,
    fwd_out,
    fwd_in,
    stat_out,
    stat_in,
    ret_out,
    ret_in,
    own_q,
    arena_k,
    arena_v,
    x_all,
    qg_all,
    w_acc,
    w_out,
    w_in,
    w_sum,
    w_fin,
    local_sem,
    table_sem,
    id_send,
    id_recv,
    fwd_send,
    fwd_recv,
    stat_send,
    stat_recv,
    ret_send,
    ret_recv,
    up_send,
    up_recv,
    down_send,
    down_recv,
    sib_send,
    sib_recv,
    qg_send,
    qg_recv,
    w_send,
    w_recv,
    f_send,
    f_recv,
):
    rows, heads, depth = q_in.shape
    topk = pick_ref.shape[1]
    scale = depth ** (-0.5)
    width = x_ref.shape[1]
    span = width // nd
    me = lax.axis_index("ctx")
    zd = lax.axis_index("dp")
    core = lax.rem(me, 2)
    chip = me // 2
    chips = nc // 2
    mine = 2 * zd + core

    def peer(j):
        return {"dp": zd, "ctx": j}

    def group_peer(t):
        return {"dp": t // 2, "ctx": 2 * chip + lax.rem(t, 2)}

    barrier = pltpu.get_barrier_semaphore()

    @pl.loop(0, nc)
    def _(j):
        @pl.when(j != me)
        def _():
            pl.semaphore_signal(barrier, inc=1, device_id=peer(j), device_id_type=MESH)

    @pl.loop(0, 2 * nd)
    def _(t):
        @pl.when(t // 2 != zd)
        def _():
            pl.semaphore_signal(barrier, inc=1, device_id=group_peer(t), device_id_type=MESH)

    def x_rows(shard, which):
        return pl.ds(pl.multiple_of((2 * shard + which) * rows, rows), rows)

    seat = pltpu.make_async_copy(x_ref, x_all.at[x_rows(zd, core)], local_sem)
    seat.start()

    lane = lax.broadcasted_iota(jnp.int32, (1, 128), 1)
    block = lax.shift_right_logical(lane, 1)
    slot = lane - 2 * block
    earlier = jnp.where(block < me, block, -1)
    ids = jnp.full((1, 128), heads, jnp.int32)
    count = jnp.zeros((1, 128), jnp.int32)
    picks = jnp.zeros((1, 128), jnp.int32)
    for e in range(heads * topk):
        target = pick_ref[e // topk, e % topk]
        hit = earlier == target
        ids = jnp.where(hit & (count == slot), e // topk, ids)
        count = count + hit.astype(jnp.int32)
        picks = jnp.where(lane == e, target, picks)
    ids_ref[...] = ids
    rank = jnp.zeros((1, 128), jnp.int32)
    for e in range(heads * topk):
        target = pick_ref[e // topk, e % topk]
        rank = rank + ((picks == target) & (lane > e)).astype(jnp.int32)
    pos_row[...] = jnp.where(picks < me, CAP * picks + rank, CAP * nc)
    tables = [
        pltpu.make_async_copy(ids_ref, head_ref, table_sem.at[0]),
        pltpu.make_async_copy(pos_row, pos_ref, table_sem.at[1]),
    ]
    for table in tables:
        table.start()

    q_ref[...] = jnp.swapaxes(q_in[...], 0, 1)
    g_ref[...] = jnp.swapaxes(g_in[...], 0, 1)
    delta = jnp.zeros((heads, rows), jnp.float32)
    for b in range(8):
        part = slice(b * rows // 8, (b + 1) * rows // 8)
        product = g_in[part].astype(jnp.float32) * o_in[part].astype(jnp.float32)
        sums = jnp.sum(product, -1, keepdims=True)
        shape = (rows // 8, heads, rows)
        token = lax.broadcasted_iota(jnp.int32, shape, 0) + b * rows // 8
        seat_of = lax.broadcasted_iota(jnp.int32, shape, 2)
        delta = delta + jnp.sum(jnp.where(token == seat_of, sums, 0.0), 0)
    delta_ref[...] = delta

    for table in tables:
        table.wait()
    seat.wait()
    pl.semaphore_wait(barrier, (nc - 1) + 2 * (nd - 1))

    lines = nc // 8

    def partner(n, sign):
        a = n % lines
        b = lax.rem(n // lines + 4 * lax.rem(a, 2), 8)
        line = lax.rem(me // 8 + sign * a + lines, lines)
        return 8 * line + lax.rem(lax.rem(me, 8) + sign * b + 8, 8)

    def id_copy(src, j, dst):
        return pltpu.make_async_remote_copy(
            src_ref=ids_ref,
            dst_ref=ids_in.at[src],
            send_sem=id_send.at[j],
            recv_sem=id_recv.at[src],
            device_id=peer(dst),
            device_id_type=MESH,
        )

    def fwd_copy(src, j, dst):
        return pltpu.make_async_remote_copy(
            src_ref=fwd_out.at[j],
            dst_ref=fwd_in.at[src],
            send_sem=fwd_send.at[j],
            recv_sem=fwd_recv.at[src],
            device_id=peer(dst),
            device_id_type=MESH,
        )

    def stat_copy(src, j, dst):
        return pltpu.make_async_remote_copy(
            src_ref=stat_out.at[j],
            dst_ref=stat_in.at[src],
            send_sem=stat_send.at[j],
            recv_sem=stat_recv.at[src],
            device_id=peer(dst),
            device_id_type=MESH,
        )

    def ret_copy(src, j, dst):
        return pltpu.make_async_remote_copy(
            src_ref=ret_out.at[j],
            dst_ref=ret_in.at[pl.ds(CAP * src, CAP)],
            send_sem=ret_send.at[j],
            recv_sem=ret_recv.at[src],
            device_id=peer(dst),
            device_id_type=MESH,
        )

    ups = nd // 2
    downs = nd - 1 - ups

    def up_copy(shard, s):
        return pltpu.make_async_remote_copy(
            src_ref=x_all.at[x_rows(shard, core)],
            dst_ref=x_all.at[x_rows(shard, core)],
            send_sem=up_send.at[s],
            recv_sem=up_recv.at[s],
            device_id={"dp": lax.rem(zd + 1, nd), "ctx": me},
            device_id_type=MESH,
        )

    def down_copy(shard, s):
        return pltpu.make_async_remote_copy(
            src_ref=x_all.at[x_rows(shard, core)],
            dst_ref=x_all.at[x_rows(shard, core)],
            send_sem=down_send.at[s],
            recv_sem=down_recv.at[s],
            device_id={"dp": lax.rem(zd + nd - 1, nd), "ctx": me},
            device_id_type=MESH,
        )

    def sib_copy(shard, which, n):
        return pltpu.make_async_remote_copy(
            src_ref=x_all.at[x_rows(shard, which)],
            dst_ref=x_all.at[x_rows(shard, which)],
            send_sem=sib_send.at[n],
            recv_sem=sib_recv.at[n],
            device_id=peer(2 * chip + 1 - core),
            device_id_type=MESH,
        )

    def below(s):
        return lax.rem(zd + nd - s, nd)

    def above(s):
        return lax.rem(zd + s, nd)

    def relay(k):
        if k == 0:
            up_copy(zd, 0).start()
            if downs:
                down_copy(zd, 0).start()
            sib_copy(zd, core, 0).start()
            return
        up_copy(below(k), k - 1).wait_recv()
        if k < ups:
            up_copy(below(k), k).start()
        sib_copy(below(k), core, k).start()
        if k <= downs:
            down_copy(above(k), k - 1).wait_recv()
            if k < downs:
                down_copy(above(k), k).start()
            sib_copy(above(k), core, ups + k).start()

    relay(0)

    @pl.loop(1, nc)
    def _(n):
        j = partner(n, -1)

        @pl.when(j < me)
        def _():
            for s in range(CAP):
                code = head_ref[0, CAP * j + s]
                alive = code < heads
                h = jnp.where(alive, code, 0)
                fwd_out[j, s, 0] = q_ref[h]
                fwd_out[j, s, 1] = g_ref[h]
                stat_out[j, pl.ds(s, 1), :] = jnp.where(alive, lse_ref[pl.ds(h, 1), :], DEAD)
                stat_out[j, pl.ds(CAP + s, 1), :] = delta_ref[pl.ds(h, 1), :]
            id_copy(me, j, j).start()
            stat_copy(me, j, j).start()
            fwd_copy(me, j, j).start()

    k_ref[...] = jnp.swapaxes(k_in[...], 0, 1)
    v_ref[...] = jnp.swapaxes(v_in[...], 0, 1)

    key_pos = lax.broadcasted_iota(jnp.int32, (rows, rows), 0)
    query_pos = lax.broadcasted_iota(jnp.int32, (rows, rows), 1)
    causal = key_pos <= query_pos

    @pl.loop(0, heads // 2)
    def _(n):
        for s in range(2):
            h = 2 * n + s
            query_part, key_part, value_part = pair_grads(
                q_ref[h],
                g_ref[h],
                k_ref[h],
                v_ref[h],
                lse_ref[pl.ds(h, 1), :],
                delta_ref[pl.ds(h, 1), :],
                scale,
                causal,
            )
            own_q[h] = query_part
            arena_k[h] = key_part
            arena_v[h] = value_part

    for h in range(heads):
        last_smem[h] = h

    @pl.loop(me + 1, nc)
    def _(i):
        id_copy(i, i, i).wait_recv()

    to_smem = pltpu.make_async_copy(ids_in, ids_smem, local_sem)
    to_smem.start()
    to_smem.wait()

    @pl.loop(1, nc)
    def _(step):
        i = partner(step, 1)

        @pl.when(i > me)
        def _():
            stat_copy(i, i, i).wait_recv()
            fwd_copy(i, i, i).wait_recv()
            for s in range(CAP):
                code = ids_smem[i, 0, CAP * me + s]
                h = jnp.where(code < heads, code, 0)
                row = heads + CAP * i + s
                query_part, key_part, value_part = pair_grads(
                    fwd_in[i, s, 0],
                    fwd_in[i, s, 1],
                    k_ref[h],
                    v_ref[h],
                    stat_in[i, pl.ds(s, 1), :],
                    stat_in[i, pl.ds(CAP + s, 1), :],
                    scale,
                )
                ret_out[i, s] = query_part.astype(jnp.bfloat16)
                before = last_smem[h]
                arena_k[row] = arena_k[before] + key_part
                arena_v[row] = arena_v[before] + value_part
                for t in range(heads):
                    last_smem[t] = jnp.where(h == t, row, last_smem[t])
            ret_copy(me, i, i).start()

        for k in range(1, ups + 1):

            @pl.when(step == max(1, k * nc // (2 * ups)))
            def _():
                relay(k)

    ret_in[CAP * nc] = jnp.zeros((rows, depth), jnp.bfloat16)

    @pl.loop(0, me)
    def _(j):
        ret_copy(j, j, j).wait_recv()

    def qg_copy(src, t, dst):
        return pltpu.make_async_remote_copy(
            src_ref=qg_ref.at[t],
            dst_ref=qg_all.at[pl.ds(pl.multiple_of(src * rows, rows), rows)],
            send_sem=qg_send.at[t],
            recv_sem=qg_recv.at[src],
            device_id=group_peer(dst),
            device_id_type=MESH,
        )

    offsets = [0]
    for k in range(1, nd // 2 + 1):
        offsets += [k] if 2 * k == nd else [k, nd - k]

    for offset in reversed(offsets):
        for which in range(2):
            h = 2 * above(offset) + which
            total = own_q[h]
            for e in range(topk):
                total = total + ret_in[pos_ref[0, topk * h + e]].astype(jnp.float32)
            qg_ref[h] = total.astype(jnp.bfloat16)
            if offset:
                qg_copy(mine, h, h).start()
            else:

                @pl.when(core != which)
                def _():
                    qg_copy(mine, h, h).start()

                @pl.when(core == which)
                def _():
                    qg_all[pl.ds(pl.multiple_of(mine * rows, rows), rows), :] = qg_ref[h]

    qg_out[...] = jnp.swapaxes(qg_ref[...], 0, 1)

    @pl.loop(0, heads)
    def _(h):
        at = last_smem[h]
        dk_ref[h] = arena_k[at].astype(jnp.bfloat16)
        dv_ref[h] = arena_v[at].astype(jnp.bfloat16)

    dk_out[...] = jnp.swapaxes(dk_ref[...], 0, 1)
    dv_out[...] = jnp.swapaxes(dv_ref[...], 0, 1)

    for n in range(nd):
        shard = zd if n == 0 else (below(n) if n <= ups else above(n - ups))
        sib_copy(shard, 1 - core, n).wait_recv()

    def add_chip(shard, r):
        tokens = pl.ds(pl.multiple_of(2 * shard * rows, 2 * rows), 2 * rows)
        columns = pl.ds(pl.multiple_of(r * span, span), span)
        return mm(qg_all[tokens, :], x_all[tokens, columns], TN)

    def w_copy(src, t, dst, half):
        part = pl.ds(half * (nd // 2), nd // 2)
        return pltpu.make_async_remote_copy(
            src_ref=w_out.at[t, part],
            dst_ref=w_in.at[src, part],
            send_sem=w_send.at[half, t],
            recv_sem=w_recv.at[half, src],
            device_id=peer(2 * dst + core),
            device_id_type=MESH,
        )

    wide = chips // lines

    def chip_partner(n, sign):
        a = n % lines
        b = lax.rem(n // lines + (wide // 2) * lax.rem(a, 2), wide)
        line = lax.rem(chip // wide + sign * a + lines, lines)
        return wide * line + lax.rem(lax.rem(chip, wide) + sign * b + wide, wide)

    for place, offset in enumerate(offsets):
        shard = above(offset)
        for which in range(2):
            t = 2 * shard + which
            if offset:
                qg_copy(t, t, t).wait_recv()
            else:

                @pl.when(core != which)
                def _():
                    qg_copy(t, t, t).wait_recv()

        if place < nd - 1:

            @pl.loop(0, nd)
            def _(r):
                part = add_chip(shard, r)
                w_acc[r] = part if place == 0 else w_acc[r] + part

            if place == 0:

                @pl.loop(0, nc)
                def _(j):
                    @pl.when(j < me)
                    def _():
                        id_copy(me, j, j).wait_send()
                        stat_copy(me, j, j).wait_send()
                        fwd_copy(me, j, j).wait_send()

                    @pl.when(j > me)
                    def _():
                        ret_copy(me, j, j).wait_send()

                for s in range(ups):
                    up_copy(zd, s).wait_send()
                for s in range(downs):
                    down_copy(zd, s).wait_send()
                for n in range(nd):
                    sib_copy(zd, core, n).wait_send()
        else:
            for half in range(2):

                @pl.loop(half * (nd // 2), (half + 1) * (nd // 2))
                def _(r):
                    part = w_acc[r] + add_chip(shard, r)
                    w_out[:, r] = part.T.astype(jnp.bfloat16).reshape(chips, span // chips, depth)

                @pl.loop(1, chips)
                def _(n):
                    t = chip_partner(n, -1)
                    w_copy(chip, t, t, half).start()

    @pl.loop(0, 2 * nd)
    def _(t):
        @pl.when(t != mine)
        def _():
            qg_copy(mine, t, t).wait_send()

    def f_copy(src, t, dst):
        return pltpu.make_async_remote_copy(
            src_ref=w_sum.at[t // 2, pl.ds(pl.multiple_of(8 * lax.rem(t, 2), 8), 8)],
            dst_ref=w_fin.at[src],
            send_sem=f_send.at[t],
            recv_sem=f_recv.at[src],
            device_id=group_peer(dst),
            device_id_type=MESH,
        )

    for half in range(2):
        part = pl.ds(half * (nd // 2), nd // 2)

        def add_part(n, total):
            t = chip_partner(n, 1)
            w_copy(t, t, t, half).wait_recv()
            return total + w_in[t, part].astype(jnp.float32)

        w_sum[part] = lax.fori_loop(1, chips, add_part, w_out[chip, part].astype(jnp.float32))

        @pl.loop(half * nd, (half + 1) * nd)
        def _(t):
            @pl.when(t != mine)
            def _():
                f_copy(mine, t, t).start()

    w_fin[mine] = w_sum[zd, pl.ds(pl.multiple_of(8 * core, 8), 8), :]

    @pl.loop(1, chips)
    def _(n):
        t = chip_partner(n, -1)
        w_copy(chip, t, t, 0).wait_send()
        w_copy(chip, t, t, 1).wait_send()

    @pl.loop(0, 2 * nd)
    def _(t):
        @pl.when(t != mine)
        def _():
            f_copy(mine, t, t).wait_send()
            f_copy(t, t, t).wait_recv()

    for t in range(2 * nd):
        wg_ref[:, t * depth : (t + 1) * depth] = w_fin[t]


def per_device(nd, nc, queries, key_rows, value_rows, attn_out, out_grad, log_sums, chosen, inputs):
    rows, heads, depth = queries.shape[1:]
    width = inputs.shape[2]
    slots = nc * CAP
    bf16, f32 = jnp.bfloat16, jnp.float32
    chips = nc // 2
    span = width // nd
    vmem = pl.BlockSpec(memory_space=pltpu.VMEM)
    smem = pl.BlockSpec(memory_space=pltpu.SMEM)
    dma = pltpu.SemaphoreType.DMA
    ups = nd // 2
    downs = nd - 1 - ups
    outs = pl.pallas_call(
        functools.partial(kernel, nd, nc),
        out_shape=(
            jax.ShapeDtypeStruct((rows, heads, depth), bf16),
            jax.ShapeDtypeStruct((rows, heads, depth), bf16),
            jax.ShapeDtypeStruct((rows, heads, depth), bf16),
            jax.ShapeDtypeStruct((8, heads * depth), f32),
        ),
        in_specs=[vmem] * 7 + [smem],
        out_specs=(vmem,) * 4,
        scratch_shapes=[pltpu.VMEM((heads, rows, depth), bf16)] * 7
        + [
            pltpu.VMEM((heads, rows), f32),
            pltpu.VMEM((1, 128), jnp.int32),
            pltpu.VMEM((1, 128), jnp.int32),
            pltpu.SMEM((1, 128), jnp.int32),
            pltpu.SMEM((1, 128), jnp.int32),
            pltpu.VMEM((nc, 1, 128), jnp.int32),
            pltpu.SMEM((nc, 1, 128), jnp.int32),
            pltpu.SMEM((heads,), jnp.int32),
            pltpu.VMEM((nc, CAP, 2, rows, depth), bf16),
            pltpu.VMEM((nc, CAP, 2, rows, depth), bf16),
            pltpu.VMEM((nc, 8, 128), f32),
            pltpu.VMEM((nc, 8, 128), f32),
            pltpu.VMEM((nc, CAP, rows, depth), bf16),
            pltpu.VMEM((slots + 1, rows, depth), bf16),
            pltpu.VMEM((heads, rows, depth), f32),
            pltpu.VMEM((heads + slots, rows, depth), f32),
            pltpu.VMEM((heads + slots, rows, depth), f32),
            pltpu.VMEM((2 * nd * rows, width), bf16),
            pltpu.VMEM((2 * nd * rows, depth), bf16),
            pltpu.VMEM((nd, depth, span), f32),
            pltpu.VMEM((chips, nd, span // chips, depth), bf16),
            pltpu.VMEM((chips, nd, span // chips, depth), bf16),
            pltpu.VMEM((nd, span // chips, depth), f32),
            pltpu.VMEM((2 * nd, 8, depth), f32),
            dma(()),
            dma((2,)),
            dma((nc,)),
            dma((nc,)),
            dma((nc,)),
            dma((nc,)),
            dma((nc,)),
            dma((nc,)),
            dma((nc,)),
            dma((nc,)),
            dma((ups,)),
            dma((ups,)),
            dma((max(downs, 1),)),
            dma((max(downs, 1),)),
            dma((nd,)),
            dma((nd,)),
            dma((2 * nd,)),
            dma((2 * nd,)),
            dma((2, chips)),
            dma((2, chips)),
            dma((2 * nd,)),
            dma((2 * nd,)),
        ],
        compiler_params=pltpu.CompilerParams(
            collective_id=0, has_side_effects=True, vmem_limit_bytes=58 * 1024 * 1024
        ),
    )(
        queries[0],
        key_rows[0],
        value_rows[0],
        attn_out[0],
        out_grad[0],
        inputs[0],
        log_sums[0],
        chosen[0, 0],
    )
    query_grad, key_grad, value_grad, weight_grad = outs
    return query_grad[None], key_grad[None], value_grad[None], weight_grad


def solution(mesh):
    nd, nc = mesh.shape["dp"], mesh.shape["ctx"]
    four = P("dp", "ctx", None, None)
    return jax.shard_map(
        functools.partial(per_device, nd, nc),
        mesh=mesh,
        in_specs=(four, four, four, four, four, P("dp", None, "ctx"), four, P("dp", "ctx", None)),
        out_specs=(four, four, four, P(("dp", "ctx"), None)),
        check_vma=False,
    )
```

```python
import functools

import jax
import jax.numpy as jnp
from jax import lax
from jax.experimental import pallas as pl
from jax.experimental.pallas import tpu as pltpu
from jax.sharding import PartitionSpec as P

CAP = 2
MESH = pl.DeviceIdType.MESH
DEAD = 1e30
AHEAD = 4
FIRST = 4
MARK = 4
STRIDE = 4
TURNS = 2
LSE_UNIT = 2.0**24
DELTA_UNIT = 2.0**18
NT = (((1,), (1,)), ((), ()))
NN = (((1,), (0,)), ((), ()))
TN = (((0,), (0,)), ((), ()))


def mm(a, b, dims):
    return lax.dot_general(a, b, dims, preferred_element_type=jnp.float32)


def pair_grads(query, grad, key, value, lse, delta, scale, keep=None):
    scores = mm(key, query, NT) * scale
    probs = jnp.exp(scores - lse)
    if keep is not None:
        probs = jnp.where(keep, probs, 0.0)
    dprobs = mm(value, grad, NT)
    dscores = (probs * (dprobs - delta)).astype(jnp.bfloat16)
    query_part = mm(dscores, key, TN) * scale
    key_part = mm(dscores, query, NN) * scale
    value_part = mm(probs.astype(jnp.bfloat16), grad, NN)
    return query_part, key_part, value_part


def kernel(
    nd,
    nc,
    q_in,
    k_in,
    v_in,
    o_in,
    g_in,
    x_ref,
    lse_ref,
    pick_ref,
    qg_out,
    dk_out,
    dv_out,
    wg_ref,
    q_ref,
    k_ref,
    v_ref,
    g_ref,
    qg_ref,
    dk_ref,
    dv_ref,
    delta_ref,
    lse_code,
    delta_own,
    ids_ref,
    pos_row,
    head_ref,
    pos_ref,
    ids_smem,
    last_smem,
    fwd_out,
    fwd_in,
    stat_out,
    stat_in,
    ret_out,
    ret_in,
    own_q,
    arena_k,
    arena_v,
    x_all,
    qg_all,
    w_acc,
    w_out,
    w_in,
    w_sum,
    w_fin,
    local_sem,
    table_sem,
    fwd_send,
    fwd_recv,
    stat_send,
    stat_recv,
    ret_send,
    ret_recv,
    up_send,
    up_recv,
    down_send,
    down_recv,
    sib_send,
    sib_recv,
    qg_send,
    qg_recv,
    hand_send,
    hand_recv,
    w_send,
    w_recv,
    f_send,
    f_recv,
):
    rows, heads, depth = q_in.shape
    topk = pick_ref.shape[1]
    scale = depth ** (-0.5)
    half_width = x_ref.shape[1] // 2
    share = nd // 2
    span = half_width // share
    me = lax.axis_index("ctx")
    zd = lax.axis_index("dp")
    core = lax.rem(me, 2)
    chip = me // 2
    chips = nc // 2

    def peer(j):
        return {"dp": zd, "ctx": j}

    barrier = pltpu.get_barrier_semaphore()

    def greet(where):
        pl.semaphore_signal(barrier, inc=1, device_id=where, device_id_type=MESH)

    for step in (1, nd - 1):
        greet({"dp": lax.rem(zd + step, nd), "ctx": me})

    @pl.when(core == 1)
    def _():
        greet(peer(me - 1))

    @pl.loop(1, nc)
    def _(n):
        i = nc - n

        @pl.when(i > me)
        def _():
            greet(peer(i))

    def x_rows(shard, which, count):
        return pl.ds(pl.multiple_of((2 * shard + which) * rows, rows), count * rows)

    def x_columns(which):
        return pl.ds(pl.multiple_of(which * half_width, half_width), half_width)

    seat = pltpu.make_async_copy(
        x_ref.at[:, x_columns(core)], x_all.at[x_rows(zd, core, 1)], local_sem
    )
    seat.start()

    lane = lax.broadcasted_iota(jnp.int32, (1, 128), 1)
    block = lax.shift_right_logical(lane, 1)
    slot = lane - 2 * block
    earlier = jnp.where(block < me, block, -1)
    ids = jnp.full((1, 128), heads, jnp.int32)
    count = jnp.zeros((1, 128), jnp.int32)
    picks = jnp.zeros((1, 128), jnp.int32)
    for e in range(heads * topk):
        target = pick_ref[e // topk, e % topk]
        hit = earlier == target
        ids = jnp.where(hit & (count == slot), e // topk, ids)
        count = count + hit.astype(jnp.int32)
        picks = jnp.where(lane == e, target, picks)
    ids_ref[...] = ids
    rank = jnp.zeros((1, 128), jnp.int32)
    for e in range(heads * topk):
        target = pick_ref[e // topk, e % topk]
        rank = rank + ((picks == target) & (lane > e)).astype(jnp.int32)
    pos_row[...] = jnp.where(picks < me, CAP * picks + rank, CAP * nc)
    tables = [
        pltpu.make_async_copy(ids_ref, head_ref, table_sem.at[0]),
        pltpu.make_async_copy(pos_row, pos_ref, table_sem.at[1]),
    ]
    for table in tables:
        table.start()

    q_ref[...] = jnp.swapaxes(q_in[...], 0, 1)
    g_ref[...] = jnp.swapaxes(g_in[...], 0, 1)
    delta = jnp.zeros((heads, rows), jnp.float32)
    for b in range(8):
        part = slice(b * rows // 8, (b + 1) * rows // 8)
        product = g_in[part].astype(jnp.float32) * o_in[part].astype(jnp.float32)
        sums = jnp.sum(product, -1, keepdims=True)
        shape = (rows // 8, heads, rows)
        token = lax.broadcasted_iota(jnp.int32, shape, 0) + b * rows // 8
        seat_of = lax.broadcasted_iota(jnp.int32, shape, 2)
        delta = delta + jnp.sum(jnp.where(token == seat_of, sums, 0.0), 0)
    delta_ref[...] = jnp.round(delta * DELTA_UNIT).astype(jnp.int32)
    lse_code[...] = jnp.round(lse_ref[...] * LSE_UNIT).astype(jnp.int32)
    delta_own[...] = delta

    for table in tables:
        table.wait()
    seat.wait()
    pl.semaphore_wait(barrier, me + 3 - core)

    lines = nc // 8

    def partner(n, sign):
        a = n % lines
        b = lax.rem(n // lines + 4 * lax.rem(a, 2), 8)
        line = lax.rem(me // 8 + sign * a + lines, lines)
        return 8 * line + lax.rem(lax.rem(me, 8) + sign * b + 8, 8)

    def fwd_copy(src, j, dst):
        return pltpu.make_async_remote_copy(
            src_ref=fwd_out.at[j],
            dst_ref=fwd_in.at[src],
            send_sem=fwd_send.at[j],
            recv_sem=fwd_recv.at[src],
            device_id=peer(dst),
            device_id_type=MESH,
        )

    def stat_copy(src, j, dst):
        return pltpu.make_async_remote_copy(
            src_ref=stat_out.at[j],
            dst_ref=stat_in.at[src],
            send_sem=stat_send.at[j],
            recv_sem=stat_recv.at[src],
            device_id=peer(dst),
            device_id_type=MESH,
        )

    def ret_copy(src, j, dst):
        return pltpu.make_async_remote_copy(
            src_ref=ret_out.at[j],
            dst_ref=ret_in.at[pl.ds(CAP * src, CAP)],
            send_sem=ret_send.at[j],
            recv_sem=ret_recv.at[src],
            device_id=peer(dst),
            device_id_type=MESH,
        )

    ups = nd // 2
    downs = nd - 1 - ups

    def ring_copy(shard, u, s, step, send_sem, recv_sem):
        piece = x_all.at[x_rows(shard, core if u == 0 else 1 - core, 1)]
        return pltpu.make_async_remote_copy(
            src_ref=piece,
            dst_ref=piece,
            send_sem=send_sem.at[s, u],
            recv_sem=recv_sem.at[s, u],
            device_id={"dp": lax.rem(zd + step, nd), "ctx": me},
            device_id_type=MESH,
        )

    def up_copy(shard, u, s):
        return ring_copy(shard, u, s, 1, up_send, up_recv)

    def down_copy(shard, u, s):
        return ring_copy(shard, u, s, nd - 1, down_send, down_recv)

    def sib_copy(which):
        return pltpu.make_async_remote_copy(
            src_ref=x_ref.at[:, x_columns(1 - core)],
            dst_ref=x_all.at[x_rows(zd, which, 1)],
            send_sem=sib_send.at[0],
            recv_sem=sib_recv.at[0],
            device_id=peer(2 * chip + 1 - core),
            device_id_type=MESH,
        )

    def below(s):
        return lax.rem(zd + nd - s, nd)

    def above(s):
        return lax.rem(zd + s, nd)

    def relay(k, u):
        if k == 0:
            if u == 1:
                sib_copy(1 - core).wait_recv()
            up_copy(zd, u, 0).start()
            if downs:
                down_copy(zd, u, 0).start()
            return
        up_copy(below(k), u, k - 1).wait_recv()
        if k < ups:
            up_copy(below(k), u, k).start()
        if k <= downs:
            down_copy(above(k), u, k - 1).wait_recv()
            if k < downs:
                down_copy(above(k), u, k).start()

    sib_copy(core).start()
    relay(0, 0)

    def send_pairs(n):
        j = partner(n, -1)

        @pl.when(j < me)
        def _():
            for s in range(CAP):
                code = head_ref[0, CAP * j + s]
                h = jnp.where(code < heads, code, 0)
                fwd_out[j, s, 0] = q_ref[h]
                fwd_out[j, s, 1] = g_ref[h]
            fwd_copy(me, j, j).start()

    @pl.loop(1, FIRST)
    def _(n):
        send_pairs(n)

    @pl.loop(1, nc)
    def _(n):
        j = partner(n, -1)

        @pl.when(j < me)
        def _():
            for s in range(CAP):
                code = head_ref[0, CAP * j + s]
                h = jnp.where(code < heads, code, 0)
                stat_out[j, pl.ds(s, 1), :] = lse_code[pl.ds(h, 1), :]
                stat_out[j, pl.ds(CAP + s, 1), :] = delta_ref[pl.ds(h, 1), :]
            stat_out[j, pl.ds(2 * CAP, 1), :] = ids_ref[...]
            stat_copy(me, j, j).start()

    relay(0, 1)

    @pl.loop(FIRST, min(AHEAD + 1, nc))
    def _(n):
        send_pairs(n)

    k_ref[...] = jnp.swapaxes(k_in[...], 0, 1)
    v_ref[...] = jnp.swapaxes(v_in[...], 0, 1)

    key_pos = lax.broadcasted_iota(jnp.int32, (rows, rows), 0)
    query_pos = lax.broadcasted_iota(jnp.int32, (rows, rows), 1)
    causal = key_pos <= query_pos

    @pl.loop(0, heads // 2)
    def _(n):
        for s in range(2):
            h = 2 * n + s
            query_part, key_part, value_part = pair_grads(
                q_ref[h],
                g_ref[h],
                k_ref[h],
                v_ref[h],
                lse_ref[pl.ds(h, 1), :],
                delta_own[pl.ds(h, 1), :],
                scale,
                causal,
            )
            own_q[h] = query_part
            arena_k[h] = key_part
            arena_v[h] = value_part

    for h in range(heads):
        last_smem[h] = h

    @pl.loop(me + 1, nc)
    def _(i):
        stat_copy(i, i, i).wait_recv()

    to_smem = pltpu.make_async_copy(stat_in.at[:, pl.ds(2 * CAP, 1)], ids_smem, local_sem)
    to_smem.start()
    to_smem.wait()

    @pl.loop(1, nc)
    def _(step):
        i = partner(step, 1)

        @pl.when(step + AHEAD < nc)
        def _():
            sent = partner(step, -1)

            @pl.when(sent < me)
            def _():
                fwd_copy(me, sent, sent).wait_send()

            send_pairs(step + AHEAD)

        @pl.when(i > me)
        def _():
            fwd_copy(i, i, i).wait_recv()
            for s in range(CAP):
                code = ids_smem[i, 0, CAP * me + s]
                alive = code < heads
                h = jnp.where(alive, code, 0)
                lse = stat_in[i, pl.ds(s, 1), :].astype(jnp.float32) * (1.0 / LSE_UNIT)
                row = heads + CAP * i + s
                query_part, key_part, value_part = pair_grads(
                    fwd_in[i, s, 0],
                    fwd_in[i, s, 1],
                    k_ref[h],
                    v_ref[h],
                    jnp.where(alive, lse, DEAD),
                    stat_in[i, pl.ds(CAP + s, 1), :].astype(jnp.float32) * (1.0 / DELTA_UNIT),
                    scale,
                )
                ret_out[i, s] = query_part.astype(jnp.bfloat16)
                before = last_smem[h]
                arena_k[row] = arena_k[before] + key_part
                arena_v[row] = arena_v[before] + value_part
                for t in range(heads):
                    last_smem[t] = jnp.where(h == t, row, last_smem[t])
            ret_copy(me, i, i).start()

        for event in range(2 * (ups - 1)):

            @pl.when(step == MARK + STRIDE * event)
            def _():
                relay(1 + event // 2, event % 2)

    ret_in[CAP * nc] = jnp.zeros((rows, depth), jnp.bfloat16)

    @pl.loop(0, me)
    def _(j):
        ret_copy(j, j, j).wait_recv()

    def qg_copy(src, shard):
        return pltpu.make_async_remote_copy(
            src_ref=qg_ref.at[pl.ds(2 * shard, 2)],
            dst_ref=qg_all.at[src, core],
            send_sem=qg_send.at[shard],
            recv_sem=qg_recv.at[src],
            device_id={"dp": shard, "ctx": me},
            device_id_type=MESH,
        )

    def hand_copy(shard, which):
        return pltpu.make_async_remote_copy(
            src_ref=qg_all.at[shard, which],
            dst_ref=qg_all.at[shard, which],
            send_sem=hand_send.at[shard],
            recv_sem=hand_recv.at[shard],
            device_id=peer(2 * chip + 1 - core),
            device_id_type=MESH,
        )

    offsets = [0]
    for k in range(1, nd // 2 + 1):
        offsets += [k] if 2 * k == nd else [k, nd - k]

    for offset in reversed(offsets):
        shard = above(offset)
        for which in range(2):
            h = 2 * shard + which
            total = own_q[h]
            for e in range(topk):
                total = total + ret_in[pos_ref[0, topk * h + e]].astype(jnp.float32)
            qg_ref[h] = total.astype(jnp.bfloat16)
        if offset:
            qg_copy(zd, shard).start()
        else:
            qg_all[zd, core] = qg_ref[pl.ds(2 * shard, 2)]
            hand_copy(zd, core).start()

    qg_out[...] = jnp.swapaxes(qg_ref[...], 0, 1)

    @pl.loop(0, heads)
    def _(h):
        at = last_smem[h]
        dk_ref[h] = arena_k[at].astype(jnp.bfloat16)
        dv_ref[h] = arena_v[at].astype(jnp.bfloat16)

    dk_out[...] = jnp.swapaxes(dk_ref[...], 0, 1)
    dv_out[...] = jnp.swapaxes(dv_ref[...], 0, 1)

    def add_chip(shard, r):
        flat = [jnp.concatenate([qg_all[shard, c, 0], qg_all[shard, c, 1]], 1) for c in range(2)]
        columns = pl.ds(pl.multiple_of(r * span, span), span)
        return mm(jnp.concatenate(flat, 0), x_all[x_rows(shard, 0, 2), columns], TN)

    turns = min(TURNS, share)
    turn_share = share // turns

    def w_copy(src, t, dst, turn):
        part = pl.ds(turn * turn_share, turn_share)
        return pltpu.make_async_remote_copy(
            src_ref=w_out.at[t, part],
            dst_ref=w_in.at[src, part],
            send_sem=w_send.at[turn, t],
            recv_sem=w_recv.at[turn, src],
            device_id=peer(2 * dst + core),
            device_id_type=MESH,
        )

    wide = chips // lines

    def chip_partner(n, sign):
        a = n % lines
        b = lax.rem(n // lines + (wide // 2) * lax.rem(a, 2), wide)
        line = lax.rem(chip // wide + sign * a + lines, lines)
        return wide * line + lax.rem(lax.rem(chip, wide) + sign * b + wide, wide)

    def hand_on(offset):
        shard = above(offset)
        qg_copy(shard, shard).wait_recv()
        hand_copy(shard, core).start()

    for place, offset in enumerate(offsets):
        shard = above(offset)
        if place + 1 < nd:
            hand_on(offsets[place + 1])
        hand_copy(shard, 1 - core).wait_recv()
        if place < nd - 1:

            @pl.loop(0, share)
            def _(r):
                part = add_chip(shard, r)
                w_acc[r] = part if place == 0 else w_acc[r] + part

            if place == 0:

                @pl.loop(0, nc)
                def _(j):
                    @pl.when(j < me)
                    def _():
                        stat_copy(me, j, j).wait_send()

                    @pl.when(j > me)
                    def _():
                        ret_copy(me, j, j).wait_send()

                @pl.loop(max(1, nc - AHEAD), nc)
                def _(n):
                    sent = partner(n, -1)

                    @pl.when(sent < me)
                    def _():
                        fwd_copy(me, sent, sent).wait_send()

                sib_copy(core).wait_send()
                for u in range(2):
                    relay(ups, u)
                    for s in range(ups):
                        up_copy(zd, u, s).wait_send()
                    for s in range(downs):
                        down_copy(zd, u, s).wait_send()
        else:
            for turn in range(turns):

                @pl.loop(turn * turn_share, (turn + 1) * turn_share)
                def _(r):
                    part = w_acc[r] + add_chip(shard, r)
                    w_out[:, r] = part.T.astype(jnp.bfloat16).reshape(chips, span // chips, 2 * depth)

                @pl.loop(1, chips)
                def _(n):
                    t = chip_partner(n, -1)
                    w_copy(chip, t, t, turn).start()

    for offset in offsets:
        if offset:
            qg_copy(zd, above(offset)).wait_send()
        hand_copy(above(offset), core).wait_send()

    def f_copy(src, q, which, shard):
        return pltpu.make_async_remote_copy(
            src_ref=w_sum.at[q, pl.ds(8 * which, 8)],
            dst_ref=w_fin.at[src],
            send_sem=f_send.at[q, which],
            recv_sem=f_recv.at[src],
            device_id={"dp": shard, "ctx": 2 * chip + which},
            device_id_type=MESH,
        )

    for turn in range(turns):
        part = pl.ds(turn * turn_share, turn_share)

        def add_part(n, total):
            t = chip_partner(n, 1)
            w_copy(t, t, t, turn).wait_recv()
            return total + w_in[t, part].astype(jnp.float32)

        w_sum[part] = lax.fori_loop(1, chips, add_part, w_out[chip, part].astype(jnp.float32))
        for q in range(turn * turn_share, (turn + 1) * turn_share):
            shard = share * core + q
            for which in range(2):
                at_home = (shard == zd) & (core == which)

                @pl.when(at_home)
                def _():
                    w_fin[zd] = w_sum[q, 8 * which : 8 * which + 8]

                @pl.when(jnp.logical_not(at_home))
                def _():
                    f_copy(zd, q, which, shard).start()

    @pl.loop(1, chips)
    def _(n):
        t = chip_partner(n, -1)
        for turn in range(turns):
            w_copy(chip, t, t, turn).wait_send()

    for q in range(share):
        shard = share * core + q
        for which in range(2):

            @pl.when((shard != zd) | (core != which))
            def _():
                f_copy(zd, q, which, shard).wait_send()

    for t in range(nd):

        @pl.when((zd != t) | (zd // share != core))
        def _():
            f_copy(t, 0, 0, 0).wait_recv()

        wg_ref[:, 2 * t * depth : 2 * (t + 1) * depth] = w_fin[t]


def per_device(nd, nc, queries, key_rows, value_rows, attn_out, out_grad, log_sums, chosen, inputs):
    rows, heads, depth = queries.shape[1:]
    width = inputs.shape[2]
    slots = nc * CAP
    bf16, f32 = jnp.bfloat16, jnp.float32
    chips = nc // 2
    share = nd // 2
    span = width // 2 // share
    vmem = pl.BlockSpec(memory_space=pltpu.VMEM)
    smem = pl.BlockSpec(memory_space=pltpu.SMEM)
    dma = pltpu.SemaphoreType.DMA
    ups = nd // 2
    downs = nd - 1 - ups
    outs = pl.pallas_call(
        functools.partial(kernel, nd, nc),
        out_shape=(
            jax.ShapeDtypeStruct((rows, heads, depth), bf16),
            jax.ShapeDtypeStruct((rows, heads, depth), bf16),
            jax.ShapeDtypeStruct((rows, heads, depth), bf16),
            jax.ShapeDtypeStruct((8, heads * depth), f32),
        ),
        in_specs=[vmem] * 7 + [smem],
        out_specs=(vmem,) * 4,
        scratch_shapes=[pltpu.VMEM((heads, rows, depth), bf16)] * 7
        + [
            pltpu.VMEM((heads, rows), jnp.int32),
            pltpu.VMEM((heads, rows), jnp.int32),
            pltpu.VMEM((heads, rows), f32),
            pltpu.VMEM((1, 128), jnp.int32),
            pltpu.VMEM((1, 128), jnp.int32),
            pltpu.SMEM((1, 128), jnp.int32),
            pltpu.SMEM((1, 128), jnp.int32),
            pltpu.SMEM((nc, 1, 128), jnp.int32),
            pltpu.SMEM((heads,), jnp.int32),
            pltpu.VMEM((nc, CAP, 2, rows, depth), bf16),
            pltpu.VMEM((nc, CAP, 2, rows, depth), bf16),
            pltpu.VMEM((nc, 8, 128), jnp.int32),
            pltpu.VMEM((nc, 8, 128), jnp.int32),
            pltpu.VMEM((nc, CAP, rows, depth), bf16),
            pltpu.VMEM((slots + 1, rows, depth), bf16),
            pltpu.VMEM((heads, rows, depth), f32),
            pltpu.VMEM((heads + slots, rows, depth), f32),
            pltpu.VMEM((heads + slots, rows, depth), f32),
            pltpu.VMEM((2 * nd * rows, width // 2), bf16),
            pltpu.VMEM((nd, 2, 2, rows, depth), bf16),
            pltpu.VMEM((share, 2 * depth, span), f32),
            pltpu.VMEM((chips, share, span // chips, 2 * depth), bf16),
            pltpu.VMEM((chips, share, span // chips, 2 * depth), bf16),
            pltpu.VMEM((share, span // chips, 2 * depth), f32),
            pltpu.VMEM((nd, 8, 2 * depth), f32),
            dma(()),
            dma((2,)),
            dma((nc,)),
            dma((nc,)),
            dma((nc,)),
            dma((nc,)),
            dma((nc,)),
            dma((nc,)),
            dma((ups, 2)),
            dma((ups, 2)),
            dma((max(downs, 1), 2)),
            dma((max(downs, 1), 2)),
            dma((1,)),
            dma((1,)),
            dma((nd,)),
            dma((nd,)),
            dma((nd,)),
            dma((nd,)),
            dma((2, chips)),
            dma((2, chips)),
            dma((share, 2)),
            dma((nd,)),
        ],
        compiler_params=pltpu.CompilerParams(
            collective_id=0, has_side_effects=True, vmem_limit_bytes=58 * 1024 * 1024
        ),
    )(
        queries[0],
        key_rows[0],
        value_rows[0],
        attn_out[0],
        out_grad[0],
        inputs[0],
        log_sums[0],
        chosen[0, 0],
    )
    query_grad, key_grad, value_grad, weight_grad = outs
    return query_grad[None], key_grad[None], value_grad[None], weight_grad


def solution(mesh):
    nd, nc = mesh.shape["dp"], mesh.shape["ctx"]
    four = P("dp", "ctx", None, None)
    return jax.shard_map(
        functools.partial(per_device, nd, nc),
        mesh=mesh,
        in_specs=(four, four, four, four, four, P("dp", None, "ctx"), four, P("dp", "ctx", None)),
        out_specs=(four, four, four, P(("dp", "ctx"), None)),
        check_vma=False,
    )
```

```python
import functools

import jax
import jax.numpy as jnp
from jax import lax
from jax.experimental import pallas as pl
from jax.experimental.pallas import tpu as pltpu
from jax.sharding import PartitionSpec as P

CAP = 2
MESH = pl.DeviceIdType.MESH
DEAD = 1e30
LEAD = 4
WINDOW = 4
PLAIN = True
FIRST = 4
MARK = 2
STRIDE = 3
TURNS = 2
LSE_UNIT = 2.0**24
DELTA_UNIT = 2.0**18
NT = (((1,), (1,)), ((), ()))
NN = (((1,), (0,)), ((), ()))
TN = (((0,), (0,)), ((), ()))


def mm(a, b, dims):
    return lax.dot_general(a, b, dims, preferred_element_type=jnp.float32)


def pair_grads(query, grad, key, value, lse, delta, scale, keep=None):
    scores = mm(key, query, NT) * scale
    probs = jnp.exp(scores - lse)
    if keep is not None:
        probs = jnp.where(keep, probs, 0.0)
    dprobs = mm(value, grad, NT)
    dscores = (probs * (dprobs - delta)).astype(jnp.bfloat16)
    query_part = mm(dscores, key, TN) * scale
    key_part = mm(dscores, query, NN) * scale
    value_part = mm(probs.astype(jnp.bfloat16), grad, NN)
    return query_part, key_part, value_part


def kernel(
    nd,
    nc,
    q_in,
    k_in,
    v_in,
    o_in,
    g_in,
    x_ref,
    lse_ref,
    pick_ref,
    qg_out,
    dk_out,
    dv_out,
    wg_ref,
    q_ref,
    k_ref,
    v_ref,
    g_ref,
    qg_ref,
    dk_ref,
    dv_ref,
    delta_ref,
    lse_code,
    delta_own,
    ids_ref,
    pos_row,
    head_ref,
    pos_ref,
    ids_smem,
    last_smem,
    fwd_out,
    fwd_in,
    stat_out,
    stat_in,
    ret_out,
    ret_in,
    own_q,
    arena_k,
    arena_v,
    x_all,
    qg_all,
    qg_flip,
    w_acc,
    w_out,
    w_in,
    w_sum,
    w_fin,
    local_sem,
    table_sem,
    fwd_send,
    fwd_recv,
    stat_send,
    stat_recv,
    ret_send,
    ret_recv,
    up_send,
    up_recv,
    down_send,
    down_recv,
    sib_send,
    sib_recv,
    qg_send,
    qg_recv,
    hand_send,
    hand_recv,
    w_send,
    w_recv,
    f_send,
    f_recv,
):
    rows, heads, depth = q_in.shape
    topk = pick_ref.shape[1]
    scale = depth ** (-0.5)
    half_width = x_ref.shape[1] // 2
    share = nd // 2
    span = half_width // share
    me = lax.axis_index("ctx")
    zd = lax.axis_index("dp")
    core = lax.rem(me, 2)
    chip = me // 2
    chips = nc // 2

    def peer(j):
        return {"dp": zd, "ctx": j}

    barrier = pltpu.get_barrier_semaphore()

    def greet(where):
        pl.semaphore_signal(barrier, inc=1, device_id=where, device_id_type=MESH)

    for step in (1, nd - 1):
        greet({"dp": lax.rem(zd + step, nd), "ctx": me})

    @pl.when(core == 1)
    def _():
        greet(peer(me - 1))

    @pl.loop(1, nc)
    def _(n):
        i = nc - n

        @pl.when(i > me)
        def _():
            greet(peer(i))

    def x_rows(shard, which, count):
        return pl.ds(pl.multiple_of((2 * shard + which) * rows, rows), count * rows)

    def x_columns(which):
        return pl.ds(pl.multiple_of(which * half_width, half_width), half_width)

    seat = pltpu.make_async_copy(
        x_ref.at[:, x_columns(core)], x_all.at[x_rows(zd, core, 1)], local_sem
    )
    seat.start()

    lane = lax.broadcasted_iota(jnp.int32, (1, 128), 1)
    block = lax.shift_right_logical(lane, 1)
    slot = lane - 2 * block
    earlier = jnp.where(block < me, block, -1)
    ids = jnp.full((1, 128), heads, jnp.int32)
    count = jnp.zeros((1, 128), jnp.int32)
    picks = jnp.zeros((1, 128), jnp.int32)
    for e in range(heads * topk):
        target = pick_ref[e // topk, e % topk]
        hit = earlier == target
        ids = jnp.where(hit & (count == slot), e // topk, ids)
        count = count + hit.astype(jnp.int32)
        picks = jnp.where(lane == e, target, picks)
    ids_ref[...] = ids
    head_table = pltpu.make_async_copy(ids_ref, head_ref, table_sem.at[0])
    head_table.start()

    q_ref[...] = jnp.swapaxes(q_in[...], 0, 1)
    g_ref[...] = jnp.swapaxes(g_in[...], 0, 1)
    head_table.wait()
    seat.wait()
    pl.semaphore_wait(barrier, me + 3 - core)

    lines = nc // 8

    def partner(n, sign):
        a = n % lines
        b = lax.rem(n // lines + 4 * lax.rem(a, 2), 8)
        line = lax.rem(me // 8 + sign * a + lines, lines)
        return 8 * line + lax.rem(lax.rem(me, 8) + sign * b + 8, 8)

    def fwd_copy(src, j, dst):
        return pltpu.make_async_remote_copy(
            src_ref=fwd_out.at[j],
            dst_ref=fwd_in.at[src],
            send_sem=fwd_send.at[j],
            recv_sem=fwd_recv.at[src],
            device_id=peer(dst),
            device_id_type=MESH,
        )

    def stat_copy(src, j, dst):
        return pltpu.make_async_remote_copy(
            src_ref=stat_out.at[j],
            dst_ref=stat_in.at[src],
            send_sem=stat_send.at[j],
            recv_sem=stat_recv.at[src],
            device_id=peer(dst),
            device_id_type=MESH,
        )

    def ret_copy(src, j, dst):
        return pltpu.make_async_remote_copy(
            src_ref=ret_out.at[j],
            dst_ref=ret_in.at[pl.ds(CAP * src, CAP)],
            send_sem=ret_send.at[j],
            recv_sem=ret_recv.at[src],
            device_id=peer(dst),
            device_id_type=MESH,
        )

    ups = nd // 2
    downs = nd - 1 - ups

    def ring_copy(shard, u, s, step, send_sem, recv_sem):
        piece = x_all.at[x_rows(shard, core if u == 0 else 1 - core, 1)]
        return pltpu.make_async_remote_copy(
            src_ref=piece,
            dst_ref=piece,
            send_sem=send_sem.at[s, u],
            recv_sem=recv_sem.at[s, u],
            device_id={"dp": lax.rem(zd + step, nd), "ctx": me},
            device_id_type=MESH,
        )

    def up_copy(shard, u, s):
        return ring_copy(shard, u, s, 1, up_send, up_recv)

    def down_copy(shard, u, s):
        return ring_copy(shard, u, s, nd - 1, down_send, down_recv)

    def sib_copy(which):
        return pltpu.make_async_remote_copy(
            src_ref=x_ref.at[:, x_columns(1 - core)],
            dst_ref=x_all.at[x_rows(zd, which, 1)],
            send_sem=sib_send.at[0],
            recv_sem=sib_recv.at[0],
            device_id=peer(2 * chip + 1 - core),
            device_id_type=MESH,
        )

    def below(s):
        return lax.rem(zd + nd - s, nd)

    def above(s):
        return lax.rem(zd + s, nd)

    def relay(k, u):
        if k == 0:
            if u == 1:
                sib_copy(1 - core).wait_recv()
            up_copy(zd, u, 0).start()
            if downs:
                down_copy(zd, u, 0).start()
            return
        up_copy(below(k), u, k - 1).wait_recv()
        if k < ups:
            up_copy(below(k), u, k).start()
        if k <= downs:
            down_copy(above(k), u, k - 1).wait_recv()
            if k < downs:
                down_copy(above(k), u, k).start()

    sib_copy(core).start()
    relay(0, 0)

    def send_pairs(n):
        j = partner(n, -1)

        @pl.when(j < me)
        def _():
            for s in range(CAP):
                code = head_ref[0, CAP * j + s]
                h = jnp.where(code < heads, code, 0)
                fwd_out[j, s, 0] = q_ref[h]
                fwd_out[j, s, 1] = g_ref[h]
            fwd_copy(me, j, j).start()

    @pl.loop(1, FIRST)
    def _(n):
        send_pairs(n)

    delta = jnp.zeros((heads, rows), jnp.float32)
    for b in range(8):
        part = slice(b * rows // 8, (b + 1) * rows // 8)
        product = g_in[part].astype(jnp.float32) * o_in[part].astype(jnp.float32)
        sums = jnp.sum(product, -1, keepdims=True)
        shape = (rows // 8, heads, rows)
        token = lax.broadcasted_iota(jnp.int32, shape, 0) + b * rows // 8
        seat_of = lax.broadcasted_iota(jnp.int32, shape, 2)
        delta = delta + jnp.sum(jnp.where(token == seat_of, sums, 0.0), 0)
    delta_ref[...] = jnp.round(delta * DELTA_UNIT).astype(jnp.int32)
    lse_code[...] = jnp.round(lse_ref[...] * LSE_UNIT).astype(jnp.int32)
    delta_own[...] = delta

    rank = jnp.zeros((1, 128), jnp.int32)
    for e in range(heads * topk):
        target = pick_ref[e // topk, e % topk]
        rank = rank + ((picks == target) & (lane > e)).astype(jnp.int32)
    pos_row[...] = jnp.where(picks < me, CAP * picks + rank, CAP * nc)
    pos_table = pltpu.make_async_copy(pos_row, pos_ref, table_sem.at[1])
    pos_table.start()

    @pl.loop(1, nc)
    def _(n):
        j = partner(n, -1)

        @pl.when(j < me)
        def _():
            for s in range(CAP):
                code = head_ref[0, CAP * j + s]
                h = jnp.where(code < heads, code, 0)
                stat_out[j, pl.ds(s, 1), :] = lse_code[pl.ds(h, 1), :]
                stat_out[j, pl.ds(CAP + s, 1), :] = delta_ref[pl.ds(h, 1), :]
            stat_out[j, pl.ds(2 * CAP, 1), :] = ids_ref[...]
            stat_copy(me, j, j).start()

    relay(0, 1)

    def paced_send(n):
        @pl.when(n > WINDOW)
        def _():
            sent = partner(n - WINDOW, -1)

            @pl.when(sent < me)
            def _():
                fwd_copy(me, sent, sent).wait_send()

        send_pairs(n)

    @pl.loop(FIRST, min(LEAD + 1, nc))
    def _(n):
        paced_send(n)

    k_ref[...] = jnp.swapaxes(k_in[...], 0, 1)
    v_ref[...] = jnp.swapaxes(v_in[...], 0, 1)

    key_pos = lax.broadcasted_iota(jnp.int32, (rows, rows), 0)
    query_pos = lax.broadcasted_iota(jnp.int32, (rows, rows), 1)
    causal = key_pos <= query_pos

    @pl.loop(0, heads // 2)
    def _(n):
        for s in range(2):
            h = 2 * n + s
            query_part, key_part, value_part = pair_grads(
                q_ref[h],
                g_ref[h],
                k_ref[h],
                v_ref[h],
                lse_ref[pl.ds(h, 1), :],
                delta_own[pl.ds(h, 1), :],
                scale,
                causal,
            )
            own_q[h] = query_part
            arena_k[h] = key_part
            arena_v[h] = value_part

    for h in range(heads):
        last_smem[h] = h

    @pl.loop(me + 1, nc)
    def _(i):
        stat_copy(i, i, i).wait_recv()

    to_smem = pltpu.make_async_copy(stat_in.at[:, pl.ds(2 * CAP, 1)], ids_smem, local_sem)
    to_smem.start()
    to_smem.wait()

    @pl.loop(1, nc)
    def _(step):
        i = partner(step, 1)

        @pl.when(step + LEAD < nc)
        def _():
            paced_send(step + LEAD)

        @pl.when(i > me)
        def _():
            fwd_copy(i, i, i).wait_recv()
            for s in range(CAP):
                code = ids_smem[i, 0, CAP * me + s]
                alive = code < heads
                h = jnp.where(alive, code, 0)
                lse = stat_in[i, pl.ds(s, 1), :].astype(jnp.float32) * (1.0 / LSE_UNIT)
                row = heads + CAP * i + s
                query_part, key_part, value_part = pair_grads(
                    fwd_in[i, s, 0],
                    fwd_in[i, s, 1],
                    k_ref[h],
                    v_ref[h],
                    jnp.where(alive, lse, DEAD),
                    stat_in[i, pl.ds(CAP + s, 1), :].astype(jnp.float32) * (1.0 / DELTA_UNIT),
                    scale,
                )
                ret_out[i, s] = query_part.astype(jnp.bfloat16)
                before = last_smem[h]
                arena_k[row] = arena_k[before] + key_part
                arena_v[row] = arena_v[before] + value_part
                for t in range(heads):
                    last_smem[t] = jnp.where(h == t, row, last_smem[t])
            ret_copy(me, i, i).start()

        for event in range(2 * (ups - 1)):

            @pl.when(step == MARK + STRIDE * event)
            def _():
                relay(1 + event // 2, event % 2)

    pos_table.wait()

    ret_in[CAP * nc] = jnp.zeros((rows, depth), jnp.bfloat16)

    @pl.loop(0, me)
    def _(j):
        ret_copy(j, j, j).wait_recv()

    def qg_copy(src, shard):
        return pltpu.make_async_remote_copy(
            src_ref=qg_ref.at[pl.ds(2 * shard, 2)],
            dst_ref=qg_all.at[src, core],
            send_sem=qg_send.at[shard],
            recv_sem=qg_recv.at[src],
            device_id={"dp": shard, "ctx": me},
            device_id_type=MESH,
        )

    def hand_copy(shard, which):
        return pltpu.make_async_remote_copy(
            src_ref=qg_all.at[shard, which],
            dst_ref=qg_all.at[shard, which],
            send_sem=hand_send.at[shard],
            recv_sem=hand_recv.at[shard],
            device_id=peer(2 * chip + 1 - core),
            device_id_type=MESH,
        )

    offsets = [0]
    for k in range(1, nd // 2 + 1):
        offsets += [k] if 2 * k == nd else [k, nd - k]

    for offset in reversed(offsets):
        shard = above(offset)
        for which in range(2):
            h = 2 * shard + which
            total = own_q[h]
            for e in range(topk):
                total = total + ret_in[pos_ref[0, topk * h + e]].astype(jnp.float32)
            qg_ref[h] = total.astype(jnp.bfloat16)
        if offset:
            qg_copy(zd, shard).start()
        else:
            qg_all[zd, core] = qg_ref[pl.ds(2 * shard, 2)]
            hand_copy(zd, core).start()

    qg_out[...] = jnp.swapaxes(qg_ref[...], 0, 1)

    @pl.loop(0, heads)
    def _(h):
        at = last_smem[h]
        dk_ref[h] = arena_k[at].astype(jnp.bfloat16)
        dv_ref[h] = arena_v[at].astype(jnp.bfloat16)

    dk_out[...] = jnp.swapaxes(dk_ref[...], 0, 1)
    dv_out[...] = jnp.swapaxes(dv_ref[...], 0, 1)

    def chip_columns(shard):
        flat = [jnp.concatenate([qg_all[shard, c, 0], qg_all[shard, c, 1]], 1) for c in range(2)]
        return jnp.concatenate(flat, 0).T

    def add_chip(flipped, shard, r):
        columns = pl.ds(pl.multiple_of(r * span, span), span)
        return mm(flipped, x_all[x_rows(shard, 0, 2), columns], NN)

    turns = min(TURNS, share)
    turn_share = share // turns

    def w_copy(src, t, dst, turn):
        part = pl.ds(turn * turn_share, turn_share)
        return pltpu.make_async_remote_copy(
            src_ref=w_out.at[t, part],
            dst_ref=w_in.at[src, part],
            send_sem=w_send.at[turn, t],
            recv_sem=w_recv.at[turn, src],
            device_id=peer(2 * dst + core),
            device_id_type=MESH,
        )

    wide = chips // lines

    def chip_partner(n, sign):
        a = n % lines
        b = lax.rem(n // lines + (wide // 2) * lax.rem(a, 2), wide)
        line = lax.rem(chip // wide + sign * a + lines, lines)
        return wide * line + lax.rem(lax.rem(chip, wide) + sign * b + wide, wide)

    def hand_on(offset):
        shard = above(offset)
        qg_copy(shard, shard).wait_recv()
        hand_copy(shard, core).start()

    for place, offset in enumerate(offsets):
        shard = above(offset)
        if place + 1 < nd:
            hand_on(offsets[place + 1])
        hand_copy(shard, 1 - core).wait_recv()
        qg_flip[...] = chip_columns(shard)
        if place < nd - 1:

            @pl.loop(0, share)
            def _(r):
                part = add_chip(qg_flip[...], shard, r)
                w_acc[r] = part if place == 0 else w_acc[r] + part

            if place == 0:

                @pl.loop(0, nc)
                def _(j):
                    @pl.when(j < me)
                    def _():
                        stat_copy(me, j, j).wait_send()

                    @pl.when(j > me)
                    def _():
                        ret_copy(me, j, j).wait_send()

                @pl.loop(max(1, nc - WINDOW), nc)
                def _(n):
                    sent = partner(n, -1)

                    @pl.when(sent < me)
                    def _():
                        fwd_copy(me, sent, sent).wait_send()

                sib_copy(core).wait_send()
                for u in range(2):
                    relay(ups, u)
                    for s in range(ups):
                        up_copy(zd, u, s).wait_send()
                    for s in range(downs):
                        down_copy(zd, u, s).wait_send()
        else:
            for turn in range(turns):

                @pl.loop(turn * turn_share, (turn + 1) * turn_share)
                def _(r):
                    part = w_acc[r] + add_chip(qg_flip[...], shard, r)
                    w_out[:, r] = part.T.astype(jnp.bfloat16).reshape(chips, span // chips, 2 * depth)

                @pl.loop(1, chips)
                def _(n):
                    t = chip_partner(n, -1)
                    w_copy(chip, t, t, turn).start()

    for offset in offsets:
        if offset:
            qg_copy(zd, above(offset)).wait_send()
        hand_copy(above(offset), core).wait_send()

    def f_copy(src, q, which, shard):
        return pltpu.make_async_remote_copy(
            src_ref=w_sum.at[q, pl.ds(8 * which, 8)],
            dst_ref=w_fin.at[src],
            send_sem=f_send.at[q, which],
            recv_sem=f_recv.at[src],
            device_id={"dp": shard, "ctx": 2 * chip + which},
            device_id_type=MESH,
        )

    for turn in range(turns):
        part = pl.ds(turn * turn_share, turn_share)

        def add_part(n, total):
            t = chip_partner(n, 1)
            w_copy(t, t, t, turn).wait_recv()
            return total + w_in[t, part].astype(jnp.float32)

        w_sum[part] = lax.fori_loop(1, chips, add_part, w_out[chip, part].astype(jnp.float32))
        for q in range(turn * turn_share, (turn + 1) * turn_share):
            shard = share * core + q
            for which in range(2):
                at_home = (shard == zd) & (core == which)

                @pl.when(at_home)
                def _():
                    w_fin[zd] = w_sum[q, 8 * which : 8 * which + 8]

                @pl.when(jnp.logical_not(at_home))
                def _():
                    f_copy(zd, q, which, shard).start()

    @pl.loop(1, chips)
    def _(n):
        t = chip_partner(n, -1)
        for turn in range(turns):
            w_copy(chip, t, t, turn).wait_send()

    for q in range(share):
        shard = share * core + q
        for which in range(2):

            @pl.when((shard != zd) | (core != which))
            def _():
                f_copy(zd, q, which, shard).wait_send()

    for t in range(nd):

        @pl.when((zd != t) | (zd // share != core))
        def _():
            f_copy(t, 0, 0, 0).wait_recv()

        wg_ref[:, 2 * t * depth : 2 * (t + 1) * depth] = w_fin[t]


def hand_over(*refs):
    count = len(refs) // 2
    for source, target in zip(refs[:count], refs[count:]):
        target[...] = source[...]


def per_device(nd, nc, queries, key_rows, value_rows, attn_out, out_grad, log_sums, chosen, inputs):
    rows, heads, depth = queries.shape[1:]
    width = inputs.shape[2]
    slots = nc * CAP
    bf16, f32 = jnp.bfloat16, jnp.float32
    chips = nc // 2
    share = nd // 2
    span = width // 2 // share
    vmem = pl.BlockSpec(memory_space=pltpu.VMEM)
    smem = pl.BlockSpec(memory_space=pltpu.SMEM)
    dma = pltpu.SemaphoreType.DMA
    ups = nd // 2
    downs = nd - 1 - ups
    outs = pl.pallas_call(
        functools.partial(kernel, nd, nc),
        out_shape=(
            jax.ShapeDtypeStruct((rows, heads, depth), bf16),
            jax.ShapeDtypeStruct((rows, heads, depth), bf16),
            jax.ShapeDtypeStruct((rows, heads, depth), bf16),
            jax.ShapeDtypeStruct((8, heads * depth), f32),
        ),
        in_specs=[vmem] * 7 + [smem],
        out_specs=(vmem,) * 4,
        scratch_shapes=[pltpu.VMEM((heads, rows, depth), bf16)] * 7
        + [
            pltpu.VMEM((heads, rows), jnp.int32),
            pltpu.VMEM((heads, rows), jnp.int32),
            pltpu.VMEM((heads, rows), f32),
            pltpu.VMEM((1, 128), jnp.int32),
            pltpu.VMEM((1, 128), jnp.int32),
            pltpu.SMEM((1, 128), jnp.int32),
            pltpu.SMEM((1, 128), jnp.int32),
            pltpu.SMEM((nc, 1, 128), jnp.int32),
            pltpu.SMEM((heads,), jnp.int32),
            pltpu.VMEM((nc, CAP, 2, rows, depth), bf16),
            pltpu.VMEM((nc, CAP, 2, rows, depth), bf16),
            pltpu.VMEM((nc, 8, 128), jnp.int32),
            pltpu.VMEM((nc, 8, 128), jnp.int32),
            pltpu.VMEM((nc, CAP, rows, depth), bf16),
            pltpu.VMEM((slots + 1, rows, depth), bf16),
            pltpu.VMEM((heads, rows, depth), f32),
            pltpu.VMEM((heads + slots, rows, depth), f32),
            pltpu.VMEM((heads + slots, rows, depth), f32),
            pltpu.VMEM((2 * nd * rows, width // 2), bf16),
            pltpu.VMEM((nd, 2, 2, rows, depth), bf16),
            pltpu.VMEM((2 * depth, 2 * rows), bf16),
            pltpu.VMEM((share, 2 * depth, span), f32),
            pltpu.VMEM((chips, share, span // chips, 2 * depth), bf16),
            pltpu.VMEM((chips, share, span // chips, 2 * depth), bf16),
            pltpu.VMEM((share, span // chips, 2 * depth), f32),
            pltpu.VMEM((nd, 8, 2 * depth), f32),
            dma(()),
            dma((2,)),
            dma((nc,)),
            dma((nc,)),
            dma((nc,)),
            dma((nc,)),
            dma((nc,)),
            dma((nc,)),
            dma((ups, 2)),
            dma((ups, 2)),
            dma((max(downs, 1), 2)),
            dma((max(downs, 1), 2)),
            dma((1,)),
            dma((1,)),
            dma((nd,)),
            dma((nd,)),
            dma((nd,)),
            dma((nd,)),
            dma((2, chips)),
            dma((2, chips)),
            dma((share, 2)),
            dma((nd,)),
        ],
        compiler_params=pltpu.CompilerParams(
            collective_id=0, has_side_effects=True, vmem_limit_bytes=58 * 1024 * 1024
        ),
    )(
        queries[0],
        key_rows[0],
        value_rows[0],
        attn_out[0],
        out_grad[0],
        inputs[0],
        log_sums[0],
        chosen[0, 0],
    )
    if PLAIN:
        outs = pl.pallas_call(
            hand_over,
            out_shape=[jax.ShapeDtypeStruct(out.shape, out.dtype) for out in outs],
            in_specs=[vmem] * 4,
            out_specs=[vmem] * 4,
        )(*outs)
    query_grad, key_grad, value_grad, weight_grad = outs
    return query_grad[None], key_grad[None], value_grad[None], weight_grad


def solution(mesh):
    nd, nc = mesh.shape["dp"], mesh.shape["ctx"]
    four = P("dp", "ctx", None, None)
    return jax.shard_map(
        functools.partial(per_device, nd, nc),
        mesh=mesh,
        in_specs=(four, four, four, four, four, P("dp", None, "ctx"), four, P("dp", "ctx", None)),
        out_specs=(four, four, four, P(("dp", "ctx"), None)),
        check_vma=False,
    )
```

```python
import functools

import jax
import jax.numpy as jnp
from jax import lax
from jax.experimental import pallas as pl
from jax.experimental.pallas import tpu as pltpu
from jax.sharding import PartitionSpec as P

CAP = 2
MESH = pl.DeviceIdType.MESH
DEAD = 1e30
LEAD = 4
WINDOW = 4
PLAIN = True
FIRST = 4
MARK = 2
STRIDE = 3
TURNS = 2
LSE_UNIT = 2.0**24
DELTA_UNIT = 2.0**18
NT = (((1,), (1,)), ((), ()))
NN = (((1,), (0,)), ((), ()))
TN = (((0,), (0,)), ((), ()))


def mm(a, b, dims):
    return lax.dot_general(a, b, dims, preferred_element_type=jnp.float32)


def pair_grads(query, grad, key, value, lse, delta, scale, keep=None):
    scores = mm(key, query, NT) * scale
    probs = jnp.exp(scores - lse)
    if keep is not None:
        probs = jnp.where(keep, probs, 0.0)
    dprobs = mm(value, grad, NT)
    dscores = (probs * (dprobs - delta)).astype(jnp.bfloat16)
    query_part = mm(dscores, key, TN) * scale
    key_part = mm(dscores, query, NN) * scale
    value_part = mm(probs.astype(jnp.bfloat16), grad, NN)
    return query_part, key_part, value_part


def kernel(
    nd,
    nc,
    q_in,
    k_in,
    v_in,
    o_in,
    g_in,
    x_ref,
    lse_ref,
    pick_ref,
    qg_out,
    dk_out,
    dv_out,
    wg_ref,
    q_ref,
    k_ref,
    v_ref,
    g_ref,
    qg_ref,
    dk_ref,
    dv_ref,
    delta_ref,
    lse_code,
    delta_own,
    ids_ref,
    pos_row,
    head_ref,
    pos_ref,
    ids_smem,
    last_smem,
    fwd_out,
    fwd_in,
    stat_out,
    stat_in,
    ret_out,
    ret_in,
    own_q,
    arena_k,
    arena_v,
    x_all,
    qg_all,
    qg_flip,
    w_acc,
    w_out,
    w_in,
    w_sum,
    w_fin,
    local_sem,
    table_sem,
    fwd_send,
    fwd_recv,
    stat_send,
    stat_recv,
    ret_send,
    ret_recv,
    up_send,
    up_recv,
    down_send,
    down_recv,
    sib_send,
    sib_recv,
    qg_send,
    qg_recv,
    hand_send,
    hand_recv,
    w_send,
    w_recv,
    f_send,
    f_recv,
):
    rows, heads, depth = q_in.shape
    topk = pick_ref.shape[0]
    scale = depth ** (-0.5)
    half_width = x_ref.shape[1] // 2
    share = nd // 2
    span = half_width // share
    me = lax.axis_index("ctx")
    zd = lax.axis_index("dp")
    core = lax.rem(me, 2)
    chip = me // 2
    chips = nc // 2

    def peer(j):
        return {"dp": zd, "ctx": j}

    barrier = pltpu.get_barrier_semaphore()

    def greet(where):
        pl.semaphore_signal(barrier, inc=1, device_id=where, device_id_type=MESH)

    for step in (1, nd - 1):
        greet({"dp": lax.rem(zd + step, nd), "ctx": me})

    @pl.when(core == 1)
    def _():
        greet(peer(me - 1))

    @pl.loop(1, nc)
    def _(n):
        i = nc - n

        @pl.when(i > me)
        def _():
            greet(peer(i))

    def x_rows(shard, which, count):
        return pl.ds(pl.multiple_of((2 * shard + which) * rows, rows), count * rows)

    def x_columns(which):
        return pl.ds(pl.multiple_of(which * half_width, half_width), half_width)

    seat = pltpu.make_async_copy(
        x_ref.at[:, x_columns(core)], x_all.at[x_rows(zd, core, 1)], local_sem
    )
    seat.start()

    lane = lax.broadcasted_iota(jnp.int32, (1, 128), 1)
    block = lax.shift_right_logical(lane, 1)
    slot = lane - 2 * block
    earlier = jnp.where(block < me, block, -1)
    ids = jnp.full((1, 128), heads, jnp.int32)
    count = jnp.zeros((1, 128), jnp.int32)
    picks = jnp.zeros((1, 128), jnp.int32)
    for e in range(heads * topk):
        target = pick_ref[e % topk, 0, e // topk]
        hit = earlier == target
        ids = jnp.where(hit & (count == slot), e // topk, ids)
        count = count + hit.astype(jnp.int32)
        picks = jnp.where(lane == e, target, picks)
    ids_ref[...] = ids
    head_table = pltpu.make_async_copy(ids_ref, head_ref, table_sem.at[0])
    head_table.start()

    q_ref[...] = jnp.swapaxes(q_in[...], 0, 1)
    g_ref[...] = jnp.swapaxes(g_in[...], 0, 1)
    head_table.wait()
    seat.wait()
    pl.semaphore_wait(barrier, me + 3 - core)

    lines = nc // 8

    def partner(n, sign):
        a = n % lines
        b = lax.rem(n // lines + 4 * lax.rem(a, 2), 8)
        line = lax.rem(me // 8 + sign * a + lines, lines)
        return 8 * line + lax.rem(lax.rem(me, 8) + sign * b + 8, 8)

    def fwd_copy(src, j, dst):
        return pltpu.make_async_remote_copy(
            src_ref=fwd_out.at[j],
            dst_ref=fwd_in.at[src],
            send_sem=fwd_send.at[j],
            recv_sem=fwd_recv.at[src],
            device_id=peer(dst),
            device_id_type=MESH,
        )

    def stat_copy(src, j, dst):
        return pltpu.make_async_remote_copy(
            src_ref=stat_out.at[j],
            dst_ref=stat_in.at[src],
            send_sem=stat_send.at[j],
            recv_sem=stat_recv.at[src],
            device_id=peer(dst),
            device_id_type=MESH,
        )

    def ret_copy(src, j, dst):
        return pltpu.make_async_remote_copy(
            src_ref=ret_out.at[j],
            dst_ref=ret_in.at[pl.ds(CAP * src, CAP)],
            send_sem=ret_send.at[j],
            recv_sem=ret_recv.at[src],
            device_id=peer(dst),
            device_id_type=MESH,
        )

    ups = nd // 2
    downs = nd - 1 - ups

    def ring_copy(shard, u, s, step, send_sem, recv_sem):
        piece = x_all.at[x_rows(shard, core if u == 0 else 1 - core, 1)]
        return pltpu.make_async_remote_copy(
            src_ref=piece,
            dst_ref=piece,
            send_sem=send_sem.at[s, u],
            recv_sem=recv_sem.at[s, u],
            device_id={"dp": lax.rem(zd + step, nd), "ctx": me},
            device_id_type=MESH,
        )

    def up_copy(shard, u, s):
        return ring_copy(shard, u, s, 1, up_send, up_recv)

    def down_copy(shard, u, s):
        return ring_copy(shard, u, s, nd - 1, down_send, down_recv)

    def sib_copy(which):
        return pltpu.make_async_remote_copy(
            src_ref=x_ref.at[:, x_columns(1 - core)],
            dst_ref=x_all.at[x_rows(zd, which, 1)],
            send_sem=sib_send.at[0],
            recv_sem=sib_recv.at[0],
            device_id=peer(2 * chip + 1 - core),
            device_id_type=MESH,
        )

    def below(s):
        return lax.rem(zd + nd - s, nd)

    def above(s):
        return lax.rem(zd + s, nd)

    def relay(k, u):
        if k == 0:
            if u == 1:
                sib_copy(1 - core).wait_recv()
            up_copy(zd, u, 0).start()
            if downs:
                down_copy(zd, u, 0).start()
            return
        up_copy(below(k), u, k - 1).wait_recv()
        if k < ups:
            up_copy(below(k), u, k).start()
        if k <= downs:
            down_copy(above(k), u, k - 1).wait_recv()
            if k < downs:
                down_copy(above(k), u, k).start()

    sib_copy(core).start()
    relay(0, 0)

    def send_pairs(n):
        j = partner(n, -1)

        @pl.when(j < me)
        def _():
            for s in range(CAP):
                code = head_ref[0, CAP * j + s]
                h = jnp.where(code < heads, code, 0)
                fwd_out[j, s, 0] = q_ref[h]
                fwd_out[j, s, 1] = g_ref[h]
            fwd_copy(me, j, j).start()

    @pl.loop(1, FIRST)
    def _(n):
        send_pairs(n)

    delta = jnp.zeros((heads, rows), jnp.float32)
    for b in range(8):
        part = slice(b * rows // 8, (b + 1) * rows // 8)
        product = g_in[part].astype(jnp.float32) * o_in[part].astype(jnp.float32)
        sums = jnp.sum(product, -1, keepdims=True)
        shape = (rows // 8, heads, rows)
        token = lax.broadcasted_iota(jnp.int32, shape, 0) + b * rows // 8
        seat_of = lax.broadcasted_iota(jnp.int32, shape, 2)
        delta = delta + jnp.sum(jnp.where(token == seat_of, sums, 0.0), 0)
    delta_ref[...] = jnp.round(delta * DELTA_UNIT).astype(jnp.int32)
    lse_code[...] = jnp.round(lse_ref[...] * LSE_UNIT).astype(jnp.int32)
    delta_own[...] = delta

    rank = jnp.zeros((1, 128), jnp.int32)
    for e in range(heads * topk):
        target = pick_ref[e % topk, 0, e // topk]
        rank = rank + ((picks == target) & (lane > e)).astype(jnp.int32)
    pos_row[...] = jnp.where(picks < me, CAP * picks + rank, CAP * nc)
    pos_table = pltpu.make_async_copy(pos_row, pos_ref, table_sem.at[1])
    pos_table.start()

    @pl.loop(1, nc)
    def _(n):
        j = partner(n, -1)

        @pl.when(j < me)
        def _():
            for s in range(CAP):
                code = head_ref[0, CAP * j + s]
                h = jnp.where(code < heads, code, 0)
                stat_out[j, pl.ds(s, 1), :] = lse_code[pl.ds(h, 1), :]
                stat_out[j, pl.ds(CAP + s, 1), :] = delta_ref[pl.ds(h, 1), :]
            stat_out[j, pl.ds(2 * CAP, 1), :] = ids_ref[...]
            stat_copy(me, j, j).start()

    relay(0, 1)

    def paced_send(n):
        @pl.when(n > WINDOW)
        def _():
            sent = partner(n - WINDOW, -1)

            @pl.when(sent < me)
            def _():
                fwd_copy(me, sent, sent).wait_send()

        send_pairs(n)

    @pl.loop(FIRST, min(LEAD + 1, nc))
    def _(n):
        paced_send(n)

    k_ref[...] = jnp.swapaxes(k_in[...], 0, 1)
    v_ref[...] = jnp.swapaxes(v_in[...], 0, 1)

    key_pos = lax.broadcasted_iota(jnp.int32, (rows, rows), 0)
    query_pos = lax.broadcasted_iota(jnp.int32, (rows, rows), 1)
    causal = key_pos <= query_pos

    @pl.loop(0, heads // 2)
    def _(n):
        for s in range(2):
            h = 2 * n + s
            query_part, key_part, value_part = pair_grads(
                q_ref[h],
                g_ref[h],
                k_ref[h],
                v_ref[h],
                lse_ref[pl.ds(h, 1), :],
                delta_own[pl.ds(h, 1), :],
                scale,
                causal,
            )
            own_q[h] = query_part
            arena_k[h] = key_part
            arena_v[h] = value_part

    for h in range(heads):
        last_smem[h] = h

    @pl.loop(me + 1, nc)
    def _(i):
        stat_copy(i, i, i).wait_recv()

    to_smem = pltpu.make_async_copy(stat_in.at[:, pl.ds(2 * CAP, 1)], ids_smem, local_sem)
    to_smem.start()
    to_smem.wait()

    @pl.loop(1, nc)
    def _(step):
        i = partner(step, 1)

        @pl.when(step + LEAD < nc)
        def _():
            paced_send(step + LEAD)

        @pl.when(i > me)
        def _():
            fwd_copy(i, i, i).wait_recv()
            for s in range(CAP):
                code = ids_smem[i, 0, CAP * me + s]
                alive = code < heads
                h = jnp.where(alive, code, 0)
                lse = stat_in[i, pl.ds(s, 1), :].astype(jnp.float32) * (1.0 / LSE_UNIT)
                row = heads + CAP * i + s
                query_part, key_part, value_part = pair_grads(
                    fwd_in[i, s, 0],
                    fwd_in[i, s, 1],
                    k_ref[h],
                    v_ref[h],
                    jnp.where(alive, lse, DEAD),
                    stat_in[i, pl.ds(CAP + s, 1), :].astype(jnp.float32) * (1.0 / DELTA_UNIT),
                    scale,
                )
                ret_out[i, s] = query_part.astype(jnp.bfloat16)
                before = last_smem[h]
                arena_k[row] = arena_k[before] + key_part
                arena_v[row] = arena_v[before] + value_part
                for t in range(heads):
                    last_smem[t] = jnp.where(h == t, row, last_smem[t])
            ret_copy(me, i, i).start()

        for event in range(2 * (ups - 1)):

            @pl.when(step == MARK + STRIDE * event)
            def _():
                relay(1 + event // 2, event % 2)

    pos_table.wait()

    ret_in[CAP * nc] = jnp.zeros((rows, depth), jnp.bfloat16)

    @pl.loop(0, me)
    def _(j):
        ret_copy(j, j, j).wait_recv()

    def qg_copy(src, shard):
        return pltpu.make_async_remote_copy(
            src_ref=qg_ref.at[pl.ds(2 * shard, 2)],
            dst_ref=qg_all.at[src, core],
            send_sem=qg_send.at[shard],
            recv_sem=qg_recv.at[src],
            device_id={"dp": shard, "ctx": me},
            device_id_type=MESH,
        )

    def hand_copy(shard, which):
        return pltpu.make_async_remote_copy(
            src_ref=qg_all.at[shard, which],
            dst_ref=qg_all.at[shard, which],
            send_sem=hand_send.at[shard],
            recv_sem=hand_recv.at[shard],
            device_id=peer(2 * chip + 1 - core),
            device_id_type=MESH,
        )

    offsets = [0]
    for k in range(1, nd // 2 + 1):
        offsets += [k] if 2 * k == nd else [k, nd - k]

    for offset in reversed(offsets):
        shard = above(offset)
        for which in range(2):
            h = 2 * shard + which
            total = own_q[h]
            for e in range(topk):
                total = total + ret_in[pos_ref[0, topk * h + e]].astype(jnp.float32)
            qg_ref[h] = total.astype(jnp.bfloat16)
        if offset:
            qg_copy(zd, shard).start()
        else:
            qg_all[zd, core] = qg_ref[pl.ds(2 * shard, 2)]
            hand_copy(zd, core).start()

    qg_out[...] = jnp.swapaxes(qg_ref[...], 0, 1)

    @pl.loop(0, heads)
    def _(h):
        at = last_smem[h]
        dk_ref[h] = arena_k[at].astype(jnp.bfloat16)
        dv_ref[h] = arena_v[at].astype(jnp.bfloat16)

    dk_out[...] = jnp.swapaxes(dk_ref[...], 0, 1)
    dv_out[...] = jnp.swapaxes(dv_ref[...], 0, 1)

    def chip_columns(shard):
        flat = [jnp.concatenate([qg_all[shard, c, 0], qg_all[shard, c, 1]], 1) for c in range(2)]
        return jnp.concatenate(flat, 0).T

    def add_chip(flipped, shard, r):
        columns = pl.ds(pl.multiple_of(r * span, span), span)
        return mm(flipped, x_all[x_rows(shard, 0, 2), columns], NN)

    turns = min(TURNS, share)
    turn_share = share // turns

    def w_copy(src, t, dst, turn):
        part = pl.ds(turn * turn_share, turn_share)
        return pltpu.make_async_remote_copy(
            src_ref=w_out.at[t, part],
            dst_ref=w_in.at[src, part],
            send_sem=w_send.at[turn, t],
            recv_sem=w_recv.at[turn, src],
            device_id=peer(2 * dst + core),
            device_id_type=MESH,
        )

    wide = chips // lines

    def chip_partner(n, sign):
        a = n % lines
        b = lax.rem(n // lines + (wide // 2) * lax.rem(a, 2), wide)
        line = lax.rem(chip // wide + sign * a + lines, lines)
        return wide * line + lax.rem(lax.rem(chip, wide) + sign * b + wide, wide)

    def hand_on(offset):
        shard = above(offset)
        qg_copy(shard, shard).wait_recv()
        hand_copy(shard, core).start()

    for place, offset in enumerate(offsets):
        shard = above(offset)
        if place + 1 < nd:
            hand_on(offsets[place + 1])
        hand_copy(shard, 1 - core).wait_recv()
        qg_flip[...] = chip_columns(shard)
        if place < nd - 1:

            @pl.loop(0, share)
            def _(r):
                part = add_chip(qg_flip[...], shard, r)
                w_acc[r] = part if place == 0 else w_acc[r] + part

            if place == 0:

                @pl.loop(0, nc)
                def _(j):
                    @pl.when(j < me)
                    def _():
                        stat_copy(me, j, j).wait_send()

                    @pl.when(j > me)
                    def _():
                        ret_copy(me, j, j).wait_send()

                @pl.loop(max(1, nc - WINDOW), nc)
                def _(n):
                    sent = partner(n, -1)

                    @pl.when(sent < me)
                    def _():
                        fwd_copy(me, sent, sent).wait_send()

                sib_copy(core).wait_send()
                for u in range(2):
                    relay(ups, u)
                    for s in range(ups):
                        up_copy(zd, u, s).wait_send()
                    for s in range(downs):
                        down_copy(zd, u, s).wait_send()
        else:
            for turn in range(turns):

                @pl.loop(turn * turn_share, (turn + 1) * turn_share)
                def _(r):
                    part = w_acc[r] + add_chip(qg_flip[...], shard, r)
                    w_out[:, r] = part.T.astype(jnp.bfloat16).reshape(chips, span // chips, 2 * depth)

                @pl.loop(1, chips)
                def _(n):
                    t = chip_partner(n, -1)
                    w_copy(chip, t, t, turn).start()

    for offset in offsets:
        if offset:
            qg_copy(zd, above(offset)).wait_send()
        hand_copy(above(offset), core).wait_send()

    def f_copy(src, q, which, shard):
        return pltpu.make_async_remote_copy(
            src_ref=w_sum.at[q, pl.ds(8 * which, 8)],
            dst_ref=w_fin.at[src],
            send_sem=f_send.at[q, which],
            recv_sem=f_recv.at[src],
            device_id={"dp": shard, "ctx": 2 * chip + which},
            device_id_type=MESH,
        )

    for turn in range(turns):
        part = pl.ds(turn * turn_share, turn_share)

        def add_part(n, total):
            t = chip_partner(n, 1)
            w_copy(t, t, t, turn).wait_recv()
            return total + w_in[t, part].astype(jnp.float32)

        w_sum[part] = lax.fori_loop(1, chips, add_part, w_out[chip, part].astype(jnp.float32))
        for q in range(turn * turn_share, (turn + 1) * turn_share):
            shard = share * core + q
            for which in range(2):
                at_home = (shard == zd) & (core == which)

                @pl.when(at_home)
                def _():
                    w_fin[zd] = w_sum[q, 8 * which : 8 * which + 8]

                @pl.when(jnp.logical_not(at_home))
                def _():
                    f_copy(zd, q, which, shard).start()

    @pl.loop(1, chips)
    def _(n):
        t = chip_partner(n, -1)
        for turn in range(turns):
            w_copy(chip, t, t, turn).wait_send()

    for q in range(share):
        shard = share * core + q
        for which in range(2):

            @pl.when((shard != zd) | (core != which))
            def _():
                f_copy(zd, q, which, shard).wait_send()

    for t in range(nd):

        @pl.when((zd != t) | (zd // share != core))
        def _():
            f_copy(t, 0, 0, 0).wait_recv()

        wg_ref[:, 2 * t * depth : 2 * (t + 1) * depth] = w_fin[t]


def hand_over(*refs):
    count = len(refs) // 2
    for source, target in zip(refs[:count], refs[count:]):
        target[...] = source[...]


def per_device(nd, nc, queries, key_rows, value_rows, attn_out, out_grad, log_sums, chosen, inputs):
    rows, heads, depth = queries.shape[1:]
    width = inputs.shape[2]
    slots = nc * CAP
    bf16, f32 = jnp.bfloat16, jnp.float32
    chips = nc // 2
    share = nd // 2
    span = width // 2 // share
    vmem = pl.BlockSpec(memory_space=pltpu.VMEM)
    smem = pl.BlockSpec(memory_space=pltpu.SMEM)
    dma = pltpu.SemaphoreType.DMA
    ups = nd // 2
    downs = nd - 1 - ups
    outs = pl.pallas_call(
        functools.partial(kernel, nd, nc),
        out_shape=(
            jax.ShapeDtypeStruct((rows, heads, depth), bf16),
            jax.ShapeDtypeStruct((rows, heads, depth), bf16),
            jax.ShapeDtypeStruct((rows, heads, depth), bf16),
            jax.ShapeDtypeStruct((8, heads * depth), f32),
        ),
        in_specs=[vmem] * 7 + [smem],
        out_specs=(vmem,) * 4,
        scratch_shapes=[pltpu.VMEM((heads, rows, depth), bf16)] * 7
        + [
            pltpu.VMEM((heads, rows), jnp.int32),
            pltpu.VMEM((heads, rows), jnp.int32),
            pltpu.VMEM((heads, rows), f32),
            pltpu.VMEM((1, 128), jnp.int32),
            pltpu.VMEM((1, 128), jnp.int32),
            pltpu.SMEM((1, 128), jnp.int32),
            pltpu.SMEM((1, 128), jnp.int32),
            pltpu.SMEM((nc, 1, 128), jnp.int32),
            pltpu.SMEM((heads,), jnp.int32),
            pltpu.VMEM((nc, CAP, 2, rows, depth), bf16),
            pltpu.VMEM((nc, CAP, 2, rows, depth), bf16),
            pltpu.VMEM((nc, 8, 128), jnp.int32),
            pltpu.VMEM((nc, 8, 128), jnp.int32),
            pltpu.VMEM((nc, CAP, rows, depth), bf16),
            pltpu.VMEM((slots + 1, rows, depth), bf16),
            pltpu.VMEM((heads, rows, depth), f32),
            pltpu.VMEM((heads + slots, rows, depth), f32),
            pltpu.VMEM((heads + slots, rows, depth), f32),
            pltpu.VMEM((2 * nd * rows, width // 2), bf16),
            pltpu.VMEM((nd, 2, 2, rows, depth), bf16),
            pltpu.VMEM((2 * depth, 2 * rows), bf16),
            pltpu.VMEM((share, 2 * depth, span), f32),
            pltpu.VMEM((chips, share, span // chips, 2 * depth), bf16),
            pltpu.VMEM((chips, share, span // chips, 2 * depth), bf16),
            pltpu.VMEM((share, span // chips, 2 * depth), f32),
            pltpu.VMEM((nd, 8, 2 * depth), f32),
            dma(()),
            dma((2,)),
            dma((nc,)),
            dma((nc,)),
            dma((nc,)),
            dma((nc,)),
            dma((nc,)),
            dma((nc,)),
            dma((ups, 2)),
            dma((ups, 2)),
            dma((max(downs, 1), 2)),
            dma((max(downs, 1), 2)),
            dma((1,)),
            dma((1,)),
            dma((nd,)),
            dma((nd,)),
            dma((nd,)),
            dma((nd,)),
            dma((2, chips)),
            dma((2, chips)),
            dma((share, 2)),
            dma((nd,)),
        ],
        compiler_params=pltpu.CompilerParams(
            collective_id=0, has_side_effects=True, vmem_limit_bytes=58 * 1024 * 1024
        ),
    )(
        queries[0],
        key_rows[0],
        value_rows[0],
        attn_out[0],
        out_grad[0],
        inputs[0],
        log_sums[0],
        jnp.transpose(chosen[0], (2, 0, 1)),
    )
    if PLAIN:
        outs = pl.pallas_call(
            hand_over,
            out_shape=[jax.ShapeDtypeStruct(out.shape, out.dtype) for out in outs],
            in_specs=[vmem] * 4,
            out_specs=[vmem] * 4,
        )(*outs)
    query_grad, key_grad, value_grad, weight_grad = outs
    return query_grad[None], key_grad[None], value_grad[None], weight_grad


def solution(mesh):
    nd, nc = mesh.shape["dp"], mesh.shape["ctx"]
    four = P("dp", "ctx", None, None)
    return jax.shard_map(
        functools.partial(per_device, nd, nc),
        mesh=mesh,
        in_specs=(four, four, four, four, four, P("dp", None, "ctx"), four, P("dp", "ctx", None)),
        out_specs=(four, four, four, P(("dp", "ctx"), None)),
        check_vma=False,
    )
```
